32 devices in a mesh: groups: 2 (over y), expert: 16 (over z, x, core).
Axes of the slice: x: 2, y: 2, z: 4, core: 2. Of those that a mesh axis runs over, the one named last changes fastest.
Arguments:
- queries: bfloat16 [192, 6144], P(('groups', 'expert')), parts along dimension 0, may hold values from -8 to 8
- tree_key_value: bfloat16 [192, 2, 1024], P(('groups', 'expert')), parts along dimension 0, may hold values from -6 to 6
- key_value_cache: bfloat16 [32, 2, 512, 1024], P(('groups', 'expert')), parts along dimension 0, may hold values from -8 to 8
- lengths: int32 [32], P(('groups', 'expert')), parts along dimension 0, may hold values from 128 to 512, as said below
- parents: int32 [192], P(('groups', 'expert')), parts along dimension 0, may hold values from 0 to 4, as said below
- residual: bfloat16 [192, 6144], P(('groups', 'expert')), parts along dimension 0, may hold values from -6 to 6
- ffn_gain: bfloat16 [6144], replicated, may hold values from 0.099609375 to 1.8984375
- router: bfloat16 [6144, 4], replicated, may hold values from -0.078125 to 0.078125
- routes: int32 [192, 2], P(('groups', 'expert')), parts along dimension 0, may hold values from 0 to 3, all different within a row; in each aligned block of 6 rows (0 to 5, 6 to 11, ...) at most 4 rows name the same one
- gate_weight: bfloat16 [6144, 32768], P(None, 'expert'), may hold values from -0.078125 to 0.078125
- up_weight: bfloat16 [6144, 32768], P(None, 'expert'), may hold values from -0.078125 to 0.078125
- down_weight: bfloat16 [32768, 6144], P('expert'), may hold values from -0.0625 to 0.0625
- accepted: int32 [32], P(('groups', 'expert')), parts along dimension 0, may hold values from 0 to 5
- next_embed: bfloat16 [32, 6144], P(('groups', 'expert')), parts along dimension 0, may hold values from -6 to 6
- draft_fc: bfloat16 [12288, 6144], P('expert'), may hold values from -0.0546875 to 0.0546875
Outputs:
- layer_out: bfloat16 [192, 6144], P(('groups', 'expert')), parts along dimension 0
- draft_out: bfloat16 [32, 6144], P(('groups', 'expert')), parts along dimension 0
The draws below stay inside these ranges and needn't reach their ends.
There are 2 independent parts, one for each index of `groups`. The reference program is written for one: setup_inputs(seed, part) draws one part's arguments, and reference() takes and returns one part's arrays. A program takes and returns all parts, laid end to end along the dimension named above; an argument that names none is the same for every part. Nothing has to cross between parts.
Inputs may be any that keep to these rules, and one draw needn't show every extreme that they name: `lengths`: both ends are reached by some request. `parents`: entry i of a request's 6 entries names an earlier node as its parent; entry 0, the root, names itself. `routes`: among the rows of one device no expert is named more than 4 times, a bound that some block reaches.
All inputs are finite; a program needn't handle non-finite values.
Results may differ from the reference program's by a relative error of at most 0.0051.
Values may be sent and summed in bfloat16 or wider, within the bound.
No kernel may reach another device: no remote copies, remote signals or barrier semaphores. Data moves between devices by JAX's collectives and lax.ppermute only.
A program may use at most 128 MiB of HBM per device.

```python
import math
import jax
import jax.numpy as jnp
import numpy as np
from jax import lax

D = 6144
QUERY_HEADS = 48
KEY_VALUE_HEADS = 8
HEAD_SIZE = 128
FF = 8192
EXPERTS = 4
TREE_NODES = 6
CACHE_SLOTS = 512
TOK_DEV = 6
CAP = 4
REQUEST_COUNT = 16
TREE_TOKENS = 96
N_EXPERT = 16


def draw_queries(key, part):
    own_key = jax.random.fold_in(key, 31)
    base_draw = jnp.clip(jax.random.normal(own_key, (TREE_TOKENS, QUERY_HEADS * HEAD_SIZE), jnp.float32), -6.0, 6.0)
    return base_draw.astype(jnp.bfloat16)


def draw_key_value_cache(key, part):
    own_key = jax.random.fold_in(key, 47)
    whole_shape = (REQUEST_COUNT, 2, CACHE_SLOTS, KEY_VALUE_HEADS * HEAD_SIZE)
    base_draw = jnp.clip(jax.random.normal(own_key, whole_shape, jnp.float32), -6.0, 6.0)
    return base_draw.astype(jnp.bfloat16)


def draw_lengths(key, part):
    first_key, second_key = jax.random.split(jax.random.fold_in(key, 5))
    drawn_lengths = jax.random.randint(first_key, (REQUEST_COUNT,), CACHE_SLOTS // 4, CACHE_SLOTS + 1)
    chosen = jax.random.randint(second_key, (), 0, REQUEST_COUNT)
    drawn_lengths = drawn_lengths.at[chosen].set(CACHE_SLOTS)
    drawn_lengths = drawn_lengths.at[(chosen + 1) % REQUEST_COUNT].set(CACHE_SLOTS // 4)
    return drawn_lengths.astype(jnp.int32)


def draw_parents(key, part):
    node_index = jnp.arange(TREE_TOKENS, dtype=jnp.int32) % TREE_NODES
    chosen = jax.random.randint(jax.random.fold_in(key, 71), (TREE_TOKENS,), 0, jnp.maximum(node_index, 1))
    chained = jnp.maximum(node_index - 1, 0)
    return jnp.where(jnp.arange(TREE_TOKENS) < TREE_NODES, chained, chosen).astype(jnp.int32)


def touch_ends(values, key, smallest, top_value):
    extent = values.shape
    index_at = [jax.random.randint(jax.random.fold_in(key, axis), (), 0, extent[axis]) for axis in range(len(extent))]
    values = values.at[tuple(index_at)].set(smallest)
    longest = extent.index(max(extent))
    index_at[longest] = (index_at[longest] + 1) % extent[longest]
    return values.at[tuple(index_at)].set(top_value)


def steps_of(rng, dims, shards, smallest, high):
    def one(position, blocks):
        steps = jax.random.uniform(jax.random.fold_in(jax.random.fold_in(rng, 6), position), (blocks,), jnp.float32, smallest / len(shards), high / len(shards))
        return jnp.repeat(jnp.exp(steps), dims[position] // blocks).reshape((-1,) + (1,) * (len(dims) - position - 1))

    loudness = one(*shards[0])
    for cut in shards[1:]:
        loudness = loudness * one(*cut)
    return loudness


def routed_block(rng, own, number, rows, number_of, top, reach, skew):
    ranking = jax.random.permutation(rng, number_of)
    packed, ordinary = load_shares(number_of, rows * top, reach, skew, True), load_shares(number_of, rows * top, reach, skew, False)
    places = jnp.arange(number_of)

    def named(tallies, offset_by):
        used = int((tallies > 0).sum())
        fixed = max(1, used // 4)
        passed = fixed + (places - fixed + offset_by * (used - fixed)) % max(1, number_of - fixed)
        return jnp.zeros((number_of,), jnp.int32).at[ranking[jnp.where(places < fixed, places, passed)]].set(jnp.asarray(tallies, jnp.int32))

    tallies = jnp.where(number % 4 == 0, named(packed, number // 4), named(ordinary, number - number // 4 - 1))
    mixed = jax.random.permutation(jax.random.fold_in(own, 3), number_of)
    source_of, taker = mixed[0:number_of // 2 * 2:2], mixed[1:number_of // 2 * 2:2]
    room = jnp.minimum(tallies[source_of] - 1, reach - tallies[taker]) // 2
    room = jnp.where((source_of == ranking[0]) | (taker == ranking[0]) | (tallies[taker] == 0), 0, jnp.maximum(room, 0))
    passed = jax.random.randint(jax.random.fold_in(own, 4), (number_of // 2,), 0, 1 << 20) % (room + 1)
    tallies = tallies.at[source_of].add(-passed).at[taker].add(passed)
    members = jnp.searchsorted(jnp.cumsum(tallies), jnp.arange(rows * top), side="right").astype(jnp.int32)
    grid = members.reshape(top, rows).T
    grid = grid[jax.random.permutation(jax.random.fold_in(own, 1), rows)]
    offset_by = jax.random.randint(jax.random.fold_in(own, 2), (rows, 1), 0, top)
    return jnp.take_along_axis(grid, (jnp.arange(top)[None, :] + offset_by) % top, axis=1)


def load_shares(number_of, total, limit, slope, full):
    weights = [(1 << 20) // math.isqrt(standing ** slope) + 1 for standing in range(1, number_of + 1)]
    largest = limit if full else min(limit, max(-(-total // number_of), total * weights[0] // sum(weights)))
    least = 1 if total - largest >= number_of - 1 else 0
    given, surplus = [largest] + [least] * (number_of - 1), total - largest - least * (number_of - 1)
    while surplus > 0:
        free = [i for i in range(1, number_of) if given[i] < largest] or [i for i in range(1, number_of) if given[i] < limit]
        mass, left = sum([weights[i] for i in free]), surplus
        for i in free:
            addition = min(limit - given[i], max(1, left * weights[i] // mass), surplus)
            given[i] = given[i] + addition
            surplus = surplus - addition
    return np.array(given)


def centred(key, dims, width, reach, cuts=(), held_as=jnp.bfloat16):
    result = width * jax.random.normal(key, dims, jnp.float32)
    if cuts:
        result = result * steps_of(key, dims, cuts, -0.22, 0.18)
    return jnp.clip(result, -reach, reach).astype(held_as)


def setup_inputs(seed: int = 0, part: int = 0) -> dict:
    key_list = jax.random.split(jax.random.key(seed), 16)
    part_splits = jax.random.split(jax.random.fold_in(key_list[15], part), 16)
    queries = draw_queries(jax.random.fold_in(jax.random.fold_in(key_list[15], part), 71), part)
    tree_key_value = centred(part_splits[1], (TREE_TOKENS, 2, KEY_VALUE_HEADS * HEAD_SIZE), 1.0, 6.0, ((0, 16),))
    key_value_cache = draw_key_value_cache(jax.random.fold_in(jax.random.fold_in(key_list[15], part), 71), part)
    lengths = draw_lengths(jax.random.fold_in(jax.random.fold_in(key_list[15], part), 71), part)
    parents = draw_parents(jax.random.fold_in(jax.random.fold_in(key_list[15], part), 71), part)
    residual = centred(part_splits[5], (TREE_TOKENS, D), 1.0, 6.0, ((0, 16),))
    ffn_gain = jnp.clip(1.0 + 0.18 * jax.random.normal(key_list[6], (D,), jnp.float32), 0.099609375, 1.8984375).astype(jnp.bfloat16)
    router = centred(key_list[7], (D, EXPERTS), D ** -0.5, 0.078125)
    routes_keys = jax.random.split(jax.random.fold_in(part_splits[8], 1), TREE_TOKENS // TOK_DEV)
    routes_turns = jax.random.permutation(jax.random.fold_in(part_splits[8], 3), TREE_TOKENS // TOK_DEV)
    routes = jax.vmap(lambda own, number: routed_block(jax.random.fold_in(part_splits[8], 2), own, number, TOK_DEV, EXPERTS, 2, CAP, 2))(routes_keys, routes_turns).reshape((TREE_TOKENS, 2))
    gate_weight = centred(key_list[9], (D, EXPERTS * FF), D ** -0.5, 0.078125, ((1, 16),))
    up_weight = centred(key_list[10], (D, EXPERTS * FF), D ** -0.5, 0.078125, ((1, 16),))
    down_weight = centred(key_list[11], (EXPERTS * FF, D), FF ** -0.5, 0.0625, ((0, 16),))
    accepted = touch_ends(jax.random.randint(part_splits[12], (REQUEST_COUNT,), 0, TREE_NODES), jax.random.fold_in(part_splits[12], 1), 0, TREE_NODES - 1).astype(jnp.int32)
    next_embed = centred(part_splits[13], (REQUEST_COUNT, D), 1.0, 6.0, ((0, 16),))
    draft_fc = centred(key_list[14], (2 * D, D), (2 * D) ** -0.5, 0.0546875, ((0, 16),))
    return dict(queries=queries, tree_key_value=tree_key_value, key_value_cache=key_value_cache, lengths=lengths, parents=parents, residual=residual, ffn_gain=ffn_gain, router=router, routes=routes, gate_weight=gate_weight, up_weight=up_weight, down_weight=down_weight, accepted=accepted, next_embed=next_embed, draft_fc=draft_fc)


EPSILON = 1e-05

def round_trip(values):
    return lax.optimization_barrier(values.astype(jnp.bfloat16)).astype(jnp.float32)

def ancestors(parent_ids):
    node_ids = jnp.arange(TREE_NODES, dtype=jnp.int32)
    parent_map = (parent_ids[:, :, None] == node_ids[None, None, :]).astype(jnp.float32)
    current = jnp.broadcast_to(jnp.eye(TREE_NODES, dtype=jnp.float32), parent_map.shape)
    reached = current
    for repeat in range(TREE_NODES):
        current = jnp.einsum('rij,rjk->rik', current, parent_map, precision=lax.Precision.HIGHEST)
        reached = reached + current
    return reached > 0.5

def attention(queries, tree_key_value, key_value_cache, lengths, parents):
    request_total = lengths.shape[0]
    query_head_count = queries.astype(jnp.float32).reshape(request_total, TREE_NODES, KEY_VALUE_HEADS, QUERY_HEADS // KEY_VALUE_HEADS, HEAD_SIZE)
    cached_key_rows = key_value_cache[:, 0].astype(jnp.float32).reshape(request_total, CACHE_SLOTS, KEY_VALUE_HEADS, HEAD_SIZE)
    cached_value_rows = key_value_cache[:, 1].astype(jnp.float32).reshape(request_total, CACHE_SLOTS, KEY_VALUE_HEADS, HEAD_SIZE)
    tree_key_rows = tree_key_value[:, 0].astype(jnp.float32).reshape(request_total, TREE_NODES, KEY_VALUE_HEADS, HEAD_SIZE)
    tree_value_rows = tree_key_value[:, 1].astype(jnp.float32).reshape(request_total, TREE_NODES, KEY_VALUE_HEADS, HEAD_SIZE)
    score_scale = HEAD_SIZE ** (-0.5)
    cache_scores = jnp.einsum('rtgqd,rlgd->rgtql', query_head_count, cached_key_rows) * score_scale
    tree_scores = jnp.einsum('rtgqd,rugd->rgtqu', query_head_count, tree_key_rows) * score_scale
    visible = jnp.arange(CACHE_SLOTS, dtype=jnp.int32)[None, :] < lengths[:, None]
    related = ancestors(parents.reshape(request_total, TREE_NODES))
    cache_scores = jnp.where(visible[:, None, None, None, :], cache_scores, -1e+30)
    tree_scores = jnp.where(related[:, None, :, None, :], tree_scores, -1e+30)
    row_peak = jnp.maximum(lax.optimization_barrier(jnp.max(cache_scores, axis=-1)), lax.optimization_barrier(jnp.max(tree_scores, axis=-1)))[..., None]
    cache_exp = jnp.exp(cache_scores - row_peak)
    tree_exp = jnp.exp(tree_scores - row_peak)
    denominator = (lax.optimization_barrier(jnp.sum(cache_exp, axis=-1)) + lax.optimization_barrier(jnp.sum(tree_exp, axis=-1)))[..., None]
    cache_weights = round_trip(cache_exp / denominator)
    tree_weights = round_trip(tree_exp / denominator)
    context = jnp.einsum('rgtql,rlgd->rtgqd', cache_weights, cached_value_rows) + jnp.einsum('rgtqu,rugd->rtgqd', tree_weights, tree_value_rows)
    return context.reshape(request_total * TREE_NODES, QUERY_HEADS * HEAD_SIZE)

def reference(queries, tree_key_value, key_value_cache, lengths, parents, residual, ffn_gain, router, routes, gate_weight, up_weight, down_weight, accepted, next_embed, draft_fc):
    context = attention(queries, tree_key_value, key_value_cache, lengths, parents)
    hidden_state = residual.astype(jnp.float32) + context
    normed = (hidden_state * lax.rsqrt(lax.optimization_barrier(jnp.mean(hidden_state * hidden_state, axis=-1, keepdims=True)) + EPSILON) * ffn_gain.astype(jnp.float32)).astype(jnp.bfloat16)
    logits = jnp.dot(normed, router, preferred_element_type=jnp.float32)
    expert_ids = jnp.arange(EXPERTS, dtype=jnp.int32)
    first_hit = (routes[:, 0:1] == expert_ids[None, :]).astype(jnp.float32)
    second_hit = (routes[:, 1:2] == expert_ids[None, :]).astype(jnp.float32)
    first_logit = lax.optimization_barrier(jnp.sum(logits * first_hit, axis=-1))
    second_logit = lax.optimization_barrier(jnp.sum(logits * second_hit, axis=-1))
    first_share = jax.nn.sigmoid(first_logit - second_logit)
    mixing = first_share[:, None] * first_hit + (1.0 - first_share)[:, None] * second_hit
    shard_width = EXPERTS * FF // N_EXPERT
    group_size = N_EXPERT // EXPERTS

    def shard_step(running, shard_index):
        first_col = (shard_index * shard_width).astype(jnp.int32)
        gate_cols = lax.dynamic_slice_in_dim(gate_weight, first_col, shard_width, 1)
        up_cols = lax.dynamic_slice_in_dim(up_weight, first_col, shard_width, 1)
        down_rows = lax.dynamic_slice_in_dim(down_weight, first_col, shard_width, 0)
        gate_val = jnp.dot(normed, gate_cols, preferred_element_type=jnp.float32)
        up_val = jnp.dot(normed, up_cols, preferred_element_type=jnp.float32)
        activation = (jax.nn.silu(gate_val) * up_val).astype(jnp.bfloat16)
        partial_out = round_trip(jnp.dot(activation, down_rows, preferred_element_type=jnp.float32))
        mix_share = lax.dynamic_slice_in_dim(mixing, (shard_index // group_size).astype(jnp.int32), 1, 1)
        return (running + mix_share * partial_out, None)
    shard_ids = jnp.arange(N_EXPERT, dtype=jnp.int32)
    expert_sum, unused = lax.scan(shard_step, jnp.zeros(hidden_state.shape, jnp.float32), shard_ids)
    layer_out = (hidden_state + expert_sum).astype(jnp.bfloat16)
    request_total = lengths.shape[0]
    picker = (accepted[:, None] == jnp.arange(TREE_NODES, dtype=jnp.int32)[None, :]).astype(jnp.float32)
    picked = jnp.einsum('rt,rtd->rd', picker, layer_out.astype(jnp.float32).reshape(request_total, TREE_NODES, D)).astype(jnp.bfloat16)
    draft_in = jnp.concatenate([picked, next_embed], axis=1)
    draft_out = jnp.dot(draft_in, draft_fc, preferred_element_type=jnp.float32).astype(jnp.bfloat16)
    return (layer_out, draft_out)
```

```python
import jax
import jax.numpy as jnp
from jax import lax
from jax.sharding import PartitionSpec as P

QUERY_HEADS = 48
KEY_VALUE_HEADS = 8
HEAD_SIZE = 128
EXPERTS = 4
TREE_NODES = 6
CACHE_SLOTS = 512
CAP = 4


EPSILON = 1e-05


def ancestors(parent_ids):
    node_ids = jnp.arange(TREE_NODES, dtype=jnp.int32)
    parent_map = (parent_ids[:, :, None] == node_ids[None, None, :]).astype(jnp.float32)
    current = jnp.broadcast_to(jnp.eye(TREE_NODES, dtype=jnp.float32), parent_map.shape)
    reached = current
    for repeat in range(TREE_NODES):
        current = jnp.einsum("rij,rjk->rik", current, parent_map, precision=lax.Precision.HIGHEST)
        reached = reached + current
    return reached > 0.5


def attention(queries, tree_key_value, key_value_cache, lengths, parents):
    request_total = lengths.shape[0]
    query_head_count = queries.reshape(
        request_total, TREE_NODES, KEY_VALUE_HEADS, QUERY_HEADS // KEY_VALUE_HEADS, HEAD_SIZE
    )
    cached_key_rows = key_value_cache[:, 0].reshape(
        request_total, CACHE_SLOTS, KEY_VALUE_HEADS, HEAD_SIZE
    )
    cached_value_rows = key_value_cache[:, 1].reshape(
        request_total, CACHE_SLOTS, KEY_VALUE_HEADS, HEAD_SIZE
    )
    tree_key_rows = tree_key_value[:, 0].reshape(
        request_total, TREE_NODES, KEY_VALUE_HEADS, HEAD_SIZE
    )
    tree_value_rows = tree_key_value[:, 1].reshape(
        request_total, TREE_NODES, KEY_VALUE_HEADS, HEAD_SIZE
    )
    score_scale = HEAD_SIZE ** (-0.5)
    cache_scores = (
        jnp.einsum(
            "rtgqd,rlgd->rgtql",
            query_head_count,
            cached_key_rows,
            preferred_element_type=jnp.float32,
        )
        * score_scale
    )
    tree_scores = (
        jnp.einsum(
            "rtgqd,rugd->rgtqu", query_head_count, tree_key_rows, preferred_element_type=jnp.float32
        )
        * score_scale
    )
    visible = jnp.arange(CACHE_SLOTS, dtype=jnp.int32)[None, :] < lengths[:, None]
    related = ancestors(parents.reshape(request_total, TREE_NODES))
    cache_scores = jnp.where(visible[:, None, None, None, :], cache_scores, -1e30)
    tree_scores = jnp.where(related[:, None, :, None, :], tree_scores, -1e30)
    row_peak = jnp.maximum(jnp.max(cache_scores, axis=-1), jnp.max(tree_scores, axis=-1))[..., None]
    cache_exp = jnp.exp(cache_scores - row_peak)
    tree_exp = jnp.exp(tree_scores - row_peak)
    denominator = (jnp.sum(cache_exp, axis=-1) + jnp.sum(tree_exp, axis=-1))[..., None]
    cache_weights = (cache_exp / denominator).astype(jnp.bfloat16)
    tree_weights = (tree_exp / denominator).astype(jnp.bfloat16)
    context = jnp.einsum(
        "rgtql,rlgd->rtgqd", cache_weights, cached_value_rows, preferred_element_type=jnp.float32
    ) + jnp.einsum(
        "rgtqu,rugd->rtgqd", tree_weights, tree_value_rows, preferred_element_type=jnp.float32
    )
    return context.reshape(request_total * TREE_NODES, QUERY_HEADS * HEAD_SIZE)


def expert_rows(rows, gate_weight, up_weight, down_weight):
    gate_val = jnp.dot(rows, gate_weight, preferred_element_type=jnp.float32)
    up_val = jnp.dot(rows, up_weight, preferred_element_type=jnp.float32)
    activation = (jax.nn.silu(gate_val) * up_val).astype(jnp.bfloat16)
    return jnp.dot(activation, down_weight, preferred_element_type=jnp.float32).astype(jnp.bfloat16)


def per_device(
    queries,
    tree_key_value,
    key_value_cache,
    lengths,
    parents,
    residual,
    ffn_gain,
    router,
    routes,
    gate_weight,
    up_weight,
    down_weight,
    accepted,
    next_embed,
    draft_fc,
):
    devices = lax.axis_size("expert")
    group_size = devices // EXPERTS
    context = attention(queries, tree_key_value, key_value_cache, lengths, parents)
    hidden_state = residual.astype(jnp.float32) + context
    normed = (
        hidden_state
        * lax.rsqrt(jnp.mean(hidden_state * hidden_state, axis=-1, keepdims=True) + EPSILON)
        * ffn_gain.astype(jnp.float32)
    ).astype(jnp.bfloat16)
    tokens_here, model_width = normed.shape
    logits = jnp.dot(normed, router, preferred_element_type=jnp.float32)
    expert_ids = jnp.arange(EXPERTS, dtype=jnp.int32)
    first_hit = (routes[:, 0:1] == expert_ids[None, :]).astype(jnp.float32)
    second_hit = (routes[:, 1:2] == expert_ids[None, :]).astype(jnp.float32)
    first_logit = jnp.sum(logits * first_hit, axis=-1)
    second_logit = jnp.sum(logits * second_hit, axis=-1)
    first_share = jax.nn.sigmoid(first_logit - second_logit)
    mixing = first_share[:, None] * first_hit + (1.0 - first_share)[:, None] * second_hit
    hit_table = first_hit + second_hit
    row_ids = jnp.arange(tokens_here, dtype=jnp.int32)
    earlier = (row_ids[None, :] < row_ids[:, None]).astype(jnp.float32)
    slot_rank = jnp.sum(earlier[:, :, None] * hit_table[None, :, :], axis=1)
    slot_ids = jnp.arange(CAP, dtype=jnp.float32)
    placing = hit_table.T[:, None, :] * (slot_rank.T[:, None, :] == slot_ids[None, :, None]).astype(
        jnp.float32
    )
    packed = jnp.einsum(
        "ect,td->ecd", placing.astype(jnp.bfloat16), normed, preferred_element_type=jnp.float32
    ).astype(jnp.bfloat16)
    outgoing = jnp.broadcast_to(packed[:, None], (EXPERTS, group_size, CAP, model_width)).reshape(
        devices, CAP, model_width
    )
    received = lax.all_to_all(outgoing, "expert", split_axis=0, concat_axis=0, tiled=True)
    flat_rows = received.reshape(-1, model_width)
    computed = expert_rows(flat_rows, gate_weight, up_weight, down_weight).reshape(received.shape)
    returned = lax.all_to_all(computed, "expert", split_axis=0, concat_axis=0, tiled=True)
    grouped = jnp.sum(
        returned.reshape(EXPERTS, group_size, CAP, model_width), axis=1, dtype=jnp.float32
    )
    weighted = placing * mixing.T[:, None, :]
    expert_sum = jnp.einsum("ect,ecd->td", weighted, grouped, precision=lax.Precision.HIGHEST)
    layer_out = (hidden_state + expert_sum).astype(jnp.bfloat16)
    request_total = lengths.shape[0]
    picker = (accepted[:, None] == jnp.arange(TREE_NODES, dtype=jnp.int32)[None, :]).astype(
        jnp.bfloat16
    )
    picked = jnp.einsum(
        "rt,rtd->rd",
        picker,
        layer_out.reshape(request_total, TREE_NODES, model_width),
        preferred_element_type=jnp.float32,
    ).astype(jnp.bfloat16)
    draft_in = jnp.concatenate([picked, next_embed], axis=1)
    columns_in = lax.all_to_all(draft_in, "expert", split_axis=1, concat_axis=0, tiled=True)
    draft_out = lax.psum_scatter(
        jnp.dot(columns_in, draft_fc, preferred_element_type=jnp.float32),
        "expert",
        scatter_dimension=0,
        tiled=True,
    ).astype(jnp.bfloat16)
    return (layer_out, draft_out)


def solution(mesh):
    return jax.shard_map(
        per_device,
        mesh=mesh,
        in_specs=(
            P(("groups", "expert"), None),
            P(("groups", "expert"), None, None),
            P(("groups", "expert"), None, None, None),
            P(("groups", "expert")),
            P(("groups", "expert")),
            P(("groups", "expert"), None),
            P(),
            P(),
            P(("groups", "expert"), None),
            P(None, "expert"),
            P(None, "expert"),
            P("expert", None),
            P(("groups", "expert")),
            P(("groups", "expert"), None),
            P("expert", None),
        ),
        out_specs=(P(("groups", "expert"), None), P(("groups", "expert"), None)),
        check_vma=False,
    )
```

```python
import functools
import jax
import jax.numpy as jnp
from jax import lax
from jax.experimental import pallas as pl
from jax.experimental.pallas import tpu as pltpu
from jax.sharding import PartitionSpec as P

QUERY_HEADS = 48
KEY_VALUE_HEADS = 8
HEAD_SIZE = 128
EXPERTS = 4
TREE_NODES = 6
CAP = 4
ROWS = 8
LANES = 128
EPSILON = 1e-05
HIDDEN = -1e30

F32 = jnp.float32
BF16 = jnp.bfloat16
VMEM = pltpu.VMEM
SMEM = pltpu.SMEM
MIB = 1 << 20


def spec(space):
    return pl.BlockSpec(memory_space=space)


def iota(shape, axis):
    return lax.broadcasted_iota(jnp.int32, shape, axis)


def along(values, shape, axis, fill=-1):
    index = iota(shape, axis)
    out = jnp.full(shape, fill, jnp.int32)
    for at, value in enumerate(values):
        out = jnp.where(index == at, value, out)
    return out


def attend(
    per_expert,
    draft_cols,
    lengths,
    parents,
    routes,
    accepted,
    queries_far,
    tree_far,
    cache,
    residual_far,
    gain_far,
    router_far,
    embed_far,
    gate,
    up,
    hidden_out,
    payload,
    placing_out,
    gate_first,
    up_first,
    queries,
    tree_key_value,
    keys,
    values,
    residual,
    gain,
    router,
    embed,
    tree,
    padded,
    hidden,
    sems,
):
    width = queries.shape[1]
    chips = payload.shape[0]
    shared = QUERY_HEADS // KEY_VALUE_HEADS
    first = gate_first.shape[1]
    moves = [
        (queries_far, queries),
        (tree_far, tree_key_value),
        (cache.at[0, 0], keys),
        (cache.at[0, 1], values),
        (residual_far, residual),
        (gain_far, gain),
        (router_far, router),
        (embed_far, embed),
        (gate.at[:, pl.ds(0, first)], gate_first),
        (up.at[:, pl.ds(0, first)], up_first),
    ]
    copies = [
        pltpu.make_async_copy(source, target, sems.at[i])
        for i, (source, target) in enumerate(moves)
    ]
    for copy in copies:
        copy.start()

    bits = []
    for t in range(TREE_NODES):
        above = jnp.int32(0)
        for j in range(t):
            above = jnp.where(parents[t] == j, bits[j], above)
        bits.append(above | (1 << t))
    counts = [jnp.int32(0)] * EXPERTS
    slots = [[], []]
    for t in range(TREE_NODES):
        for k in range(2):
            slot = jnp.int32(0)
            for e in range(EXPERTS):
                slot = jnp.where(routes[k, t] == e, e * CAP + counts[e], slot)
            slots[k].append(slot)
        for e in range(EXPERTS):
            named = jnp.logical_or(routes[0, t] == e, routes[1, t] == e)
            counts[e] = counts[e] + named.astype(jnp.int32)

    tree[...] = jnp.zeros(tree.shape, F32)
    copies[0].wait()
    copies[1].wait()
    for t in range(TREE_NODES):
        pair = tree_key_value[t].astype(F32)
        tree[0, t : t + 1, :] = pair[0:1]
        tree[1, t : t + 1, :] = pair[1:2]
    padded[...] = jnp.zeros(padded.shape, F32)
    padded[0:TREE_NODES, :] = queries[...].astype(F32)

    slots_total = keys.shape[0]
    visible = iota((shared * ROWS, slots_total), 1) < lengths[0]
    row = iota((shared * ROWS, ROWS), 0) & (ROWS - 1)
    row_bits = jnp.ones((shared * ROWS, ROWS), jnp.int32)
    for t in range(TREE_NODES):
        row_bits = jnp.where(row == t, bits[t], row_bits)
    related = ((row_bits >> iota((shared * ROWS, ROWS), 1)) & 1) == 1
    scale = HEAD_SIZE ** (-0.5)
    contract_last = (((1,), (1,)), ((), ()))
    for copy in copies[2:8]:
        copy.wait()
    hidden[...] = jnp.zeros(hidden.shape, F32)
    hidden[0:TREE_NODES, :] = residual[...].astype(F32)
    for g in range(KEY_VALUE_HEADS):
        head = slice(g * HEAD_SIZE, (g + 1) * HEAD_SIZE)
        block = jnp.concatenate(
            [
                padded[:, (g * shared + i) * HEAD_SIZE : (g * shared + i + 1) * HEAD_SIZE]
                for i in range(shared)
            ],
            axis=0,
        ).astype(BF16)
        cache_scores = (
            lax.dot_general(block, keys[:, head], contract_last, preferred_element_type=F32)
            * scale
        )
        tree_scores = (
            lax.dot_general(
                block, tree[0, :, head].astype(BF16), contract_last, preferred_element_type=F32
            )
            * scale
        )
        cache_scores = jnp.where(visible, cache_scores, HIDDEN)
        tree_scores = jnp.where(related, tree_scores, HIDDEN)
        peak = jnp.maximum(
            jnp.max(cache_scores, axis=1, keepdims=True),
            jnp.max(tree_scores, axis=1, keepdims=True),
        )
        cache_exp = jnp.exp(cache_scores - peak)
        tree_exp = jnp.exp(tree_scores - peak)
        total = jnp.sum(cache_exp, axis=1, keepdims=True) + jnp.sum(
            tree_exp, axis=1, keepdims=True
        )
        share = 1.0 / total
        context = jnp.dot(
            (cache_exp * share).astype(BF16), values[:, head], preferred_element_type=F32
        ) + jnp.dot(
            (tree_exp * share).astype(BF16),
            tree[1, :, head].astype(BF16),
            preferred_element_type=F32,
        )
        for i in range(shared):
            columns = slice((g * shared + i) * HEAD_SIZE, (g * shared + i + 1) * HEAD_SIZE)
            hidden[:, columns] = hidden[:, columns] + context[i * ROWS : (i + 1) * ROWS]

    state = hidden[...]
    hidden_out[...] = state
    mean = jnp.sum(state * state, axis=1, keepdims=True) * (1.0 / width)
    gains = gain[...].astype(F32)
    shrink = lax.rsqrt(mean + EPSILON)
    normed = jnp.concatenate(
        [
            state[:, i * LANES : (i + 1) * LANES] * shrink * gains[i : i + 1]
            for i in range(width // LANES)
        ],
        axis=1,
    ).astype(BF16)
    logits = lax.dot_general(normed, router[...], contract_last, preferred_element_type=F32)
    expert = iota((ROWS, EXPERTS), 1)
    route = [
        along([routes[k, t] for t in range(TREE_NODES)], (ROWS, EXPERTS), 0) for k in range(2)
    ]
    picked_logit = [
        jnp.sum(jnp.where(expert == route[k], logits, 0.0), axis=1, keepdims=True)
        for k in range(2)
    ]
    first = jax.nn.sigmoid(picked_logit[0] - picked_logit[1])
    lane = iota((ROWS, LANES), 1)
    is_accepted = (iota((ROWS, LANES), 0) == accepted[0]).astype(F32)
    extras = []
    for weight in (first, 1.0 - first):
        high = weight.astype(BF16).astype(F32)
        extras.append(
            jnp.where(
                lane == 0,
                high,
                jnp.where(lane == 1, weight - high, jnp.where(lane == 2, is_accepted, 0.0)),
            ).astype(BF16)
        )
    place_row = iota((EXPERTS * ROWS, ROWS), 0)
    target = (place_row // ROWS) * CAP + (place_row & (ROWS - 1))
    target = jnp.where((place_row & (ROWS - 1)) < CAP, target, -2)
    hits = [
        (target == along(slots[k], (EXPERTS * ROWS, ROWS), 1)).astype(F32).astype(BF16)
        for k in range(2)
    ]
    packed = jnp.dot(hits[0] + hits[1], normed, preferred_element_type=F32)
    extra = jnp.dot(hits[0], extras[0], preferred_element_type=F32) + jnp.dot(
        hits[1], extras[1], preferred_element_type=F32
    )
    for e in range(EXPERTS):
        rows = packed[e * ROWS : e * ROWS + CAP].astype(BF16)
        last = extra[e * ROWS : e * ROWS + CAP].astype(BF16)
        for q in range(e * per_expert, (e + 1) * per_expert):
            payload[q, :, 0:width] = rows
            payload[q, :, payload.shape[2] - LANES :] = last
    if draft_cols:
        chosen = jnp.sum(
            jnp.where(iota((ROWS, width), 0) == accepted[0], state, 0.0), axis=0, keepdims=True
        )
        rest = embed[...].astype(F32)
        for q in range(chips):
            for i in range(CAP):
                at = (q * CAP + i) * draft_cols
                source = chosen if at < width else rest
                at = at % width
                payload[q, i : i + 1, width : width + draft_cols] = source[
                    :, at : at + draft_cols
                ].astype(BF16)
    lane_slot = iota(placing_out.shape, 1)
    lane_slot = (lane_slot // (CAP * per_expert)) * CAP + lane_slot % CAP
    placing_out[...] = jnp.logical_or(
        lane_slot == along(slots[0], placing_out.shape, 0),
        lane_slot == along(slots[1], placing_out.shape, 0),
    ).astype(F32)
    for copy in copies[8:]:
        copy.wait()


def experts(
    width,
    mine,
    other,
    gate_first,
    up_first,
    gate,
    up,
    down,
    keep,
    send,
    notes,
    weights,
    rows,
    acts,
    gates,
    ups,
    downs,
    gate_sems,
    up_sems,
    down_sems,
):
    chips, _, whole_width = mine.shape
    half = chips * CAP
    first = gate_first.shape[1]
    buffers, _, chunk = gates.shape
    down_buffers, hidden_units, step = downs.shape
    chunks = (hidden_units - first) // chunk
    steps = width // step

    def gate_copies(i):
        columns = pl.ds(first + i * chunk, chunk)
        slot = i % buffers
        return (
            pltpu.make_async_copy(gate.at[:, columns], gates.at[slot], gate_sems.at[slot]),
            pltpu.make_async_copy(up.at[:, columns], ups.at[slot], up_sems.at[slot]),
        )

    def down_copy(i):
        slot = i % down_buffers
        return pltpu.make_async_copy(
            down.at[:, pl.ds(i * step, step)], downs.at[slot], down_sems.at[slot]
        )

    queue = [copy for i in range(chunks) for copy in gate_copies(i)]
    queue += [down_copy(i) for i in range(steps)]
    ahead = 2 * buffers

    def issue(upto):
        nonlocal issued
        while issued < min(upto, len(queue)):
            queue[issued].start()
            issued += 1

    issued = 0
    issue(ahead)
    group = 16 // CAP
    for side, source in enumerate((mine, other)):
        for q in range(0, chips, group):
            at = slice(side * half + q * CAP, side * half + (q + group) * CAP)
            full = jnp.concatenate(
                [source[q + i].astype(F32) for i in range(group)], axis=0
            )
            rows[at, :] = full[:, 0:width].astype(BF16)
            notes[at, :] = full[:, width : whole_width - LANES].astype(BF16)
            weights[at, :] = full[:, whole_width - LANES :]

    def activate(gate_block, up_block, at):
        gate_val = jnp.dot(rows[...], gate_block, preferred_element_type=F32)
        up_val = jnp.dot(rows[...], up_block, preferred_element_type=F32)
        acts[:, at : at + gate_block.shape[1]] = (
            gate_val / (1.0 + jnp.exp(-gate_val)) * up_val
        ).astype(BF16)

    for at in range(0, first, chunk):
        activate(gate_first[:, at : at + chunk], up_first[:, at : at + chunk], at)
    for i in range(chunks):
        for copy in gate_copies(i):
            copy.wait()
        slot = i % buffers
        activate(gates[slot], ups[slot], first + i * chunk)
        if i + buffers < chunks:
            issue(ahead + 2 * (i + 1))
        else:
            issue(2 * chunks + (i + buffers - chunks + 1) * down_buffers // buffers)
    mix = weights[:, 0:1] + weights[:, 1:2]
    for i in range(steps):
        down_copy(i).wait()
        result = jnp.dot(acts[...], downs[i % down_buffers], preferred_element_type=F32) * mix
        columns = slice(i * step, (i + 1) * step)
        keep[:, columns] = result[:half]
        send[:, columns] = result[half:].astype(BF16)
        issue(2 * chunks + down_buffers + i + 1)


def combine(draft_cols, keep, came, flags, returned, draft):
    chips = returned.shape[0]
    width = keep.shape[1]
    total = keep[...] + came[...].astype(F32)
    for q in range(chips):
        returned[q] = total[q * CAP : (q + 1) * CAP].astype(BF16)
    row = iota((chips * CAP, chips), 0)
    select = jnp.where(row // CAP == iota((chips * CAP, chips), 1), flags[0 : chips * CAP, 2:3], 0.0)
    chosen = lax.dot_general(
        select.astype(BF16),
        total.astype(BF16),
        (((0,), (0,)), ((), ())),
        preferred_element_type=F32,
    ).astype(BF16)
    if draft_cols:
        for d in range(draft.shape[0]):
            if d * draft_cols < width:
                draft[d] = chosen[:, d * draft_cols : (d + 1) * draft_cols]
            else:
                draft[d] = jnp.zeros(draft.shape[1:], BF16)
    else:
        draft[...] = chosen


def project(came, notes, fc, out, near, spread, sems):
    devices, requests, columns = came.shape
    chips = devices // 2
    half = chips * CAP
    pieces, step = out.shape[1:]
    copies = [
        pltpu.make_async_copy(
            fc.at[:, pl.ds(i * step, step)], near.at[:, pl.ds(i * step, step)], sems.at[i]
        )
        for i in range(pieces)
    ]
    for copy in copies:
        copy.start()
    core = lax.axis_index("expert") % 2
    row = iota((chips, half), 0)
    col = iota((chips, half), 1)
    sides = []
    for side in range(2):
        stacked = notes[side * half : (side + 1) * half, : 2 * columns // CAP]
        flat = jnp.concatenate(
            [
                jnp.dot(
                    (col == row * CAP + i).astype(F32).astype(BF16),
                    stacked,
                    preferred_element_type=F32,
                )
                for i in range(CAP)
            ],
            axis=1,
        )
        sides.append(jnp.where(core == 0, flat[:, :columns], flat[:, columns:]))
    inputs = []
    for c in range(2):
        total = jnp.where(core == 0, sides[c], sides[1 - c])
        for q in range(chips):
            total = total + came[2 * q + c].astype(F32)
        inputs.append(total)
    inputs = jnp.concatenate(inputs, axis=0).astype(BF16)
    for i in range(pieces):
        copies[i].wait()
        result = jnp.dot(
            inputs, near[:, i * step : (i + 1) * step], preferred_element_type=F32
        )
        for k in range(step // LANES):
            spread[k, pl.ds(i, devices, stride=pieces), :] = result[
                :, k * LANES : (k + 1) * LANES
            ]
    for c in range(2):
        for q in range(chips):
            at = (c * chips + q) * pieces
            for k in range(step // LANES):
                out[2 * q + c, :, k * LANES : (k + 1) * LANES] = spread[
                    k, at : at + pieces, :
                ].astype(BF16)


def finish(came, out):
    total = came[0].astype(F32)
    for d in range(1, came.shape[0]):
        total = total + came[d].astype(F32)
    step = total.shape[1]
    for i in range(total.shape[0]):
        out[:, i * step : (i + 1) * step] = total[i : i + 1].astype(BF16)


def settle(hidden, placing, came, out):
    chips = came.shape[0]
    rows = jnp.concatenate([came[q].astype(F32) for q in range(chips)], axis=0).astype(BF16)
    total = hidden[...] + jnp.dot(
        placing[...].astype(BF16), rows, preferred_element_type=F32
    )
    out[...] = total[: out.shape[0]].astype(BF16)


def far(array):
    return pltpu.with_memory_space_constraint(array, pltpu.HBM)


def near(array):
    return pltpu.with_memory_space_constraint(array, VMEM)


def params(mib):
    return pltpu.CompilerParams(vmem_limit_bytes=mib * MIB)


def per_device(
    queries,
    tree_key_value,
    key_value_cache,
    lengths,
    parents,
    residual,
    ffn_gain,
    router,
    routes,
    gate_weight,
    up_weight,
    down_weight,
    accepted,
    next_embed,
    draft_fc,
):
    devices = lax.axis_size("expert")
    chips = devices // 2
    per_expert = chips // EXPERTS
    tokens, width = queries.shape
    assert lengths.shape[0] == 1 and tokens == TREE_NODES
    cache_slots, key_width = key_value_cache.shape[2:]
    hidden_units = gate_weight.shape[1]
    draft_rows = draft_fc.shape[0]
    aligned = (2 * draft_rows) % (CAP * LANES) == 0
    ext = 2 * draft_rows // CAP
    ext_pad = -(-ext // LANES) * LANES
    total_width = width + ext_pad + LANES
    same_core = [[2 * q + c for q in range(chips)] for c in range(2)]
    swap = [(d, d ^ 1) for d in range(devices)]

    first = 512 if hidden_units > 1024 else hidden_units // 2
    chunk = min(256, first)
    hidden, payload, placing, gate_first, up_first = pl.pallas_call(
        functools.partial(attend, per_expert, ext if aligned else 0),
        out_shape=(
            jax.ShapeDtypeStruct((ROWS, width), F32),
            jax.ShapeDtypeStruct((chips, CAP, total_width), BF16),
            jax.ShapeDtypeStruct((ROWS, chips * CAP), F32),
            VMEM((width, first), BF16),
            VMEM((width, first), BF16),
        ),
        in_specs=[spec(SMEM)] * 4 + [spec(pl.ANY)] * 9,
        out_specs=(spec(VMEM),) * 5,
        scratch_shapes=[
            VMEM(queries.shape, BF16),
            VMEM(tree_key_value.shape, BF16),
            VMEM((cache_slots, key_width), BF16),
            VMEM((cache_slots, key_width), BF16),
            VMEM(residual.shape, BF16),
            VMEM((width // LANES, LANES), BF16),
            VMEM((EXPERTS, width), BF16),
            VMEM(next_embed.shape, BF16),
            VMEM((2, ROWS, key_width), F32),
            VMEM((ROWS, width), F32),
            VMEM((ROWS, width), F32),
            pltpu.SemaphoreType.DMA((10,)),
        ],
        compiler_params=params(12),
    )(
        lengths,
        parents,
        routes.T,
        accepted,
        far(queries),
        far(tree_key_value),
        far(key_value_cache),
        far(residual),
        far(ffn_gain.reshape(width // LANES, LANES)),
        far(router.T),
        far(next_embed),
        far(gate_weight),
        far(up_weight),
    )
    if not aligned:
        chosen = lax.dynamic_slice_in_dim(hidden, accepted[0], 1, 0)
        early_cols = jnp.concatenate([chosen.astype(BF16), next_embed], axis=1)
        early_cols = early_cols.reshape(chips, CAP, ext)
        early_cols = jnp.pad(early_cols, ((0, 0), (0, 0), (0, ext_pad - ext)))
        payload = lax.dynamic_update_slice(payload, early_cols, (0, 0, width))

    mine = lax.all_to_all(
        payload, "expert", 0, 0, tiled=True, axis_index_groups=same_core
    )
    other = lax.ppermute(mine, "expert", swap)
    step = 512
    buffers, down_buffers = 3, 6
    rows = 2 * chips * CAP
    keep, send, notes, weights = pl.pallas_call(
        functools.partial(experts, width),
        out_shape=(
            VMEM((chips * CAP, width), F32),
            VMEM((chips * CAP, width), BF16),
            VMEM((rows, ext_pad), BF16),
            VMEM((rows, LANES), F32),
        ),
        in_specs=[spec(VMEM)] * 4 + [spec(pl.ANY)] * 3,
        out_specs=(spec(VMEM),) * 4,
        scratch_shapes=[
            VMEM((rows, width), BF16),
            VMEM((rows, hidden_units), BF16),
            VMEM((buffers, width, chunk), BF16),
            VMEM((buffers, width, chunk), BF16),
            VMEM((down_buffers, hidden_units, step), BF16),
            pltpu.SemaphoreType.DMA((buffers,)),
            pltpu.SemaphoreType.DMA((buffers,)),
            pltpu.SemaphoreType.DMA((down_buffers,)),
        ],
        compiler_params=params(40),
        cost_estimate=pl.CostEstimate(
            flops=2 * rows * width * hidden_units * 3,
            bytes_accessed=3 * down_weight.size * 2,
            transcendentals=0,
        ),
    )(
        near(mine),
        near(other),
        near(gate_first),
        near(up_first),
        far(gate_weight),
        far(up_weight),
        far(down_weight),
    )
    came = lax.ppermute(send, "expert", swap)
    draft_shape = (devices, chips, draft_rows) if aligned else (chips, width)
    partial, draft = pl.pallas_call(
        functools.partial(combine, draft_rows if aligned else 0),
        out_shape=(
            jax.ShapeDtypeStruct((chips, CAP, width), BF16),
            jax.ShapeDtypeStruct(draft_shape, BF16),
        ),
        in_specs=[spec(VMEM)] * 3,
        out_specs=(spec(VMEM),) * 2,
        compiler_params=params(12 if aligned else 40),
    )(near(keep), came, near(weights))
    if not aligned:
        draft = draft.reshape(chips, devices // 2, draft_rows).transpose(1, 0, 2)
        draft = jnp.concatenate([draft, jnp.zeros_like(draft)], axis=0)
    draft_came = lax.all_to_all(draft, "expert", 0, 0, tiled=True)
    returned = lax.all_to_all(
        partial, "expert", 0, 0, tiled=True, axis_index_groups=same_core
    )
    sums = pl.pallas_call(
        project,
        out_shape=jax.ShapeDtypeStruct((devices, ROWS, width // ROWS), BF16),
        in_specs=[spec(VMEM)] * 2 + [spec(pl.ANY)],
        out_specs=spec(VMEM),
        scratch_shapes=[
            VMEM(draft_fc.shape, BF16),
            VMEM((width // ROWS // LANES, devices * ROWS, LANES), F32),
            pltpu.SemaphoreType.DMA((ROWS,)),
        ],
        compiler_params=params(24),
    )(draft_came, notes, far(draft_fc))
    sums_came = lax.all_to_all(sums, "expert", 0, 0, tiled=True)
    layer_out = pl.pallas_call(
        settle,
        out_shape=jax.ShapeDtypeStruct((tokens, width), BF16),
        in_specs=[spec(VMEM)] * 3,
        out_specs=spec(VMEM),
        compiler_params=params(16),
    )(hidden, placing, returned)
    draft_out = pl.pallas_call(
        finish,
        out_shape=jax.ShapeDtypeStruct((1, width), BF16),
        in_specs=[spec(VMEM)],
        out_specs=spec(VMEM),
        compiler_params=params(8),
    )(sums_came)
    return (layer_out, draft_out)


def solution(mesh):
    return jax.shard_map(
        per_device,
        mesh=mesh,
        in_specs=(
            P(("groups", "expert"), None),
            P(("groups", "expert"), None, None),
            P(("groups", "expert"), None, None, None),
            P(("groups", "expert")),
            P(("groups", "expert")),
            P(("groups", "expert"), None),
            P(),
            P(),
            P(("groups", "expert"), None),
            P(None, "expert"),
            P(None, "expert"),
            P("expert", None),
            P(("groups", "expert")),
            P(("groups", "expert"), None),
            P("expert", None),
        ),
        out_specs=(P(("groups", "expert"), None), P(("groups", "expert"), None)),
        check_vma=False,
    )
```

```python
import functools
import jax
import jax.numpy as jnp
from jax import lax
from jax.experimental import pallas as pl
from jax.experimental.pallas import tpu as pltpu
from jax.sharding import PartitionSpec as P

QUERY_HEADS = 48
KEY_VALUE_HEADS = 8
HEAD_SIZE = 128
EXPERTS = 4
TREE_NODES = 6
CAP = 4
ROWS = 8
LANES = 128
EPSILON = 1e-05
HIDDEN = -1e30

F32 = jnp.float32
BF16 = jnp.bfloat16
VMEM = pltpu.VMEM
SMEM = pltpu.SMEM
MIB = 1 << 20


def spec(space):
    return pl.BlockSpec(memory_space=space)


def iota(shape, axis):
    return lax.broadcasted_iota(jnp.int32, shape, axis)


def along(values, shape, axis, fill=-1):
    index = iota(shape, axis)
    out = jnp.full(shape, fill, jnp.int32)
    for at, value in enumerate(values):
        out = jnp.where(index == at, value, out)
    return out


def attend(
    lengths,
    accepted,
    parents_far,
    routes_far,
    queries_far,
    tree_far,
    cache,
    residual_far,
    gain_far,
    router_far,
    embed_far,
    gate,
    up,
    hidden_out,
    send_0,
    send_1,
    send_2,
    send_3,
    placing_out,
    gate_first,
    up_first,
    parents,
    routes,
    queries,
    tree_key_value,
    keys,
    values,
    residual,
    gain,
    router,
    embed,
    tree,
    padded,
    hidden,
    payload,
    sems,
):
    width = queries.shape[1]
    per_expert = placing_out.shape[1] // (CAP * EXPERTS)
    draft_cols = payload.shape[2] - width - LANES
    shared = QUERY_HEADS // KEY_VALUE_HEADS
    first = gate_first.shape[1]
    moves = [
        (parents_far, parents),
        (routes_far, routes),
        (queries_far, queries),
        (tree_far, tree_key_value),
        (cache.at[0, 0], keys),
        (cache.at[0, 1], values),
        (residual_far, residual),
        (gain_far, gain),
        (router_far, router),
        (embed_far, embed),
        (gate.at[:, pl.ds(0, first)], gate_first),
        (up.at[:, pl.ds(0, first)], up_first),
    ]
    copies = [
        pltpu.make_async_copy(source, target, sems.at[i])
        for i, (source, target) in enumerate(moves)
    ]
    for copy in copies:
        copy.start()
    for copy in copies[:2]:
        copy.wait()

    bits = []
    for t in range(TREE_NODES):
        above = jnp.int32(0)
        for j in range(t):
            above = jnp.where(parents[t] == j, bits[j], above)
        bits.append(above | (1 << t))
    counts = [jnp.int32(0)] * EXPERTS
    slots = [[], []]
    for t in range(TREE_NODES):
        for k in range(2):
            slot = jnp.int32(0)
            for e in range(EXPERTS):
                slot = jnp.where(routes[k, t] == e, e * CAP + counts[e], slot)
            slots[k].append(slot)
        for e in range(EXPERTS):
            named = jnp.logical_or(routes[0, t] == e, routes[1, t] == e)
            counts[e] = counts[e] + named.astype(jnp.int32)

    tree[...] = jnp.zeros(tree.shape, F32)
    copies[2].wait()
    copies[3].wait()
    for t in range(TREE_NODES):
        pair = tree_key_value[t].astype(F32)
        tree[0, t : t + 1, :] = pair[0:1]
        tree[1, t : t + 1, :] = pair[1:2]
    padded[...] = jnp.zeros(padded.shape, F32)
    padded[0:TREE_NODES, :] = queries[...].astype(F32)

    slots_total = keys.shape[0]
    visible = iota((shared * ROWS, slots_total), 1) < lengths[0]
    row = iota((shared * ROWS, ROWS), 0) & (ROWS - 1)
    row_bits = jnp.ones((shared * ROWS, ROWS), jnp.int32)
    for t in range(TREE_NODES):
        row_bits = jnp.where(row == t, bits[t], row_bits)
    related = ((row_bits >> iota((shared * ROWS, ROWS), 1)) & 1) == 1
    scale = HEAD_SIZE ** (-0.5)
    contract_last = (((1,), (1,)), ((), ()))
    for copy in copies[4:10]:
        copy.wait()
    hidden[...] = jnp.zeros(hidden.shape, F32)
    hidden[0:TREE_NODES, :] = residual[...].astype(F32)
    for g in range(KEY_VALUE_HEADS):
        head = slice(g * HEAD_SIZE, (g + 1) * HEAD_SIZE)
        block = jnp.concatenate(
            [
                padded[:, (g * shared + i) * HEAD_SIZE : (g * shared + i + 1) * HEAD_SIZE]
                for i in range(shared)
            ],
            axis=0,
        ).astype(BF16)
        cache_scores = (
            lax.dot_general(block, keys[:, head], contract_last, preferred_element_type=F32)
            * scale
        )
        tree_scores = (
            lax.dot_general(
                block, tree[0, :, head].astype(BF16), contract_last, preferred_element_type=F32
            )
            * scale
        )
        cache_scores = jnp.where(visible, cache_scores, HIDDEN)
        tree_scores = jnp.where(related, tree_scores, HIDDEN)
        peak = jnp.maximum(
            jnp.max(cache_scores, axis=1, keepdims=True),
            jnp.max(tree_scores, axis=1, keepdims=True),
        )
        cache_exp = jnp.exp(cache_scores - peak)
        tree_exp = jnp.exp(tree_scores - peak)
        total = jnp.sum(cache_exp, axis=1, keepdims=True) + jnp.sum(
            tree_exp, axis=1, keepdims=True
        )
        share = 1.0 / total
        context = jnp.dot(
            (cache_exp * share).astype(BF16), values[:, head], preferred_element_type=F32
        ) + jnp.dot(
            (tree_exp * share).astype(BF16),
            tree[1, :, head].astype(BF16),
            preferred_element_type=F32,
        )
        for i in range(shared):
            columns = slice((g * shared + i) * HEAD_SIZE, (g * shared + i + 1) * HEAD_SIZE)
            hidden[:, columns] = hidden[:, columns] + context[i * ROWS : (i + 1) * ROWS]

    state = hidden[...]
    hidden_out[...] = state
    mean = jnp.sum(state * state, axis=1, keepdims=True) * (1.0 / width)
    gains = gain[...].astype(F32)
    shrink = lax.rsqrt(mean + EPSILON)
    normed = jnp.concatenate(
        [
            state[:, i * LANES : (i + 1) * LANES] * shrink * gains[i : i + 1]
            for i in range(width // LANES)
        ],
        axis=1,
    ).astype(BF16)
    logits = lax.dot_general(normed, router[...], contract_last, preferred_element_type=F32)
    expert = iota((ROWS, EXPERTS), 1)
    route = [
        along([routes[k, t] for t in range(TREE_NODES)], (ROWS, EXPERTS), 0) for k in range(2)
    ]
    picked_logit = [
        jnp.sum(jnp.where(expert == route[k], logits, 0.0), axis=1, keepdims=True)
        for k in range(2)
    ]
    first = jax.nn.sigmoid(picked_logit[0] - picked_logit[1])
    lane = iota((ROWS, LANES), 1)
    is_accepted = (iota((ROWS, LANES), 0) == accepted[0]).astype(F32)
    extras = []
    for weight in (first, 1.0 - first):
        high = weight.astype(BF16).astype(F32)
        extras.append(
            jnp.where(
                lane == 0,
                high,
                jnp.where(lane == 1, weight - high, jnp.where(lane == 2, is_accepted, 0.0)),
            ).astype(BF16)
        )
    place_row = iota((EXPERTS * ROWS, ROWS), 0)
    target = (place_row // ROWS) * CAP + (place_row & (ROWS - 1))
    target = jnp.where((place_row & (ROWS - 1)) < CAP, target, -2)
    hits = [
        (target == along(slots[k], (EXPERTS * ROWS, ROWS), 1)).astype(F32).astype(BF16)
        for k in range(2)
    ]
    packed = jnp.dot(hits[0] + hits[1], normed, preferred_element_type=F32)
    extra = jnp.dot(hits[0], extras[0], preferred_element_type=F32) + jnp.dot(
        hits[1], extras[1], preferred_element_type=F32
    )
    for e in range(EXPERTS):
        rows = packed[e * ROWS : e * ROWS + CAP].astype(BF16)
        last = extra[e * ROWS : e * ROWS + CAP].astype(BF16)
        payload[e, :, 0:width] = rows
        payload[e, :, width + draft_cols :] = last
    chosen = jnp.sum(
        jnp.where(iota((ROWS, width), 0) == accepted[0], state, 0.0), axis=0, keepdims=True
    )
    rest = embed[...].astype(F32)
    for e in range(EXPERTS):
        for i in range(CAP):
            at = (e * CAP + i) * draft_cols
            source = chosen if at < width else rest
            at = at % width
            payload[e, i : i + 1, width : width + draft_cols] = source[
                :, at : at + draft_cols
            ].astype(BF16)
    mine = lax.axis_index("expert") // (2 * per_expert)
    for shift, target in enumerate((send_0, send_1, send_2, send_3)):
        target[...] = payload[lax.rem(mine + shift, EXPERTS)]
    lane_slot = iota(placing_out.shape, 1)
    lane_slot = (lane_slot // (CAP * per_expert)) * CAP + lane_slot % CAP
    placing_out[...] = jnp.logical_or(
        lane_slot == along(slots[0], placing_out.shape, 0),
        lane_slot == along(slots[1], placing_out.shape, 0),
    ).astype(F32)
    for copy in copies[10:]:
        copy.wait()


def fetch(first, after, gate, up, gate_next, up_next, sems):
    del after
    columns = pl.ds(first, gate_next.shape[1])
    copies = [
        pltpu.make_async_copy(gate.at[:, columns], gate_next, sems.at[0]),
        pltpu.make_async_copy(up.at[:, columns], up_next, sems.at[1]),
    ]
    for copy in copies:
        copy.start()
    for copy in copies:
        copy.wait()


def join(*refs):
    for i, ref in enumerate(refs[:-1]):
        refs[-1][i] = ref[...]


def experts(width, sources, held, *refs):
    pieces, refs = refs[:sources], refs[sources:]
    ready, refs = refs[: 2 * held], refs[2 * held :]
    stream(width, pieces, ready, *refs)


def stream(
    width,
    pieces,
    ready,
    gate,
    up,
    down,
    keep,
    send,
    notes,
    weights,
    rows,
    acts,
    units,
    sems,
):
    whole_width = pieces[0].shape[2]
    half = keep.shape[0]
    count, depth, chunk = units.shape
    first = sum(block.shape[1] for block in ready[::2])
    parts = width // depth
    queue = []
    spans = [(at, min(chunk, depth - at)) for at in range(first, depth, chunk)]
    for at, span in spans:
        for source in (gate, up):
            for p in range(parts):
                queue.append((source.at[pl.ds(p * depth, depth), pl.ds(at, span)], span))
    for at in range(0, width, chunk):
        queue.append((down.at[:, pl.ds(at, chunk)], chunk))
    copies = [
        pltpu.make_async_copy(
            source, units.at[i % count, :, pl.ds(0, span)], sems.at[i % count]
        )
        for i, (source, span) in enumerate(queue)
    ]
    for copy in copies[:count]:
        copy.start()
    taken = 0

    def product(left):
        nonlocal taken
        copies[taken].wait()
        span = queue[taken][1]
        result = jnp.dot(
            left, units[taken % count, :, 0:span], preferred_element_type=F32
        )
        if taken + count < len(copies):
            copies[taken + count].start()
        taken += 1
        return result

    for k, source in enumerate(pieces):
        at = slice(k * EXPERTS * CAP, (k + 1) * EXPERTS * CAP)
        full = jnp.concatenate([source[z].astype(F32) for z in range(EXPERTS)], axis=0)
        rows[at, :] = full[:, 0:width].astype(BF16)
        notes[at, :] = full[:, width : whole_width - LANES].astype(BF16)
        weights[at, :] = full[:, whole_width - LANES :]
    if rows.shape[0] > 2 * half:
        rows[2 * half :, :] = jnp.zeros((rows.shape[0] - 2 * half, width), BF16)

    def activate(gate_val, up_val, at):
        acts[:, at : at + gate_val.shape[1]] = (
            gate_val / (1.0 + jnp.exp(-gate_val)) * up_val
        ).astype(BF16)

    base = 0
    for gate_block, up_block in zip(ready[::2], ready[1::2]):
        activate(
            jnp.dot(rows[...], gate_block[...], preferred_element_type=F32),
            jnp.dot(rows[...], up_block[...], preferred_element_type=F32),
            base,
        )
        base += gate_block.shape[1]
    for at, _ in spans:
        gate_val, up_val = [
            sum(product(rows[:, p * depth : (p + 1) * depth]) for p in range(parts))
            for _ in range(2)
        ]
        activate(gate_val, up_val, at)
    mix = weights[:, 0:1] + weights[:, 1:2]
    for at in range(0, width, chunk):
        result = product(acts[...])[: 2 * half] * mix
        keep[:, at : at + chunk] = result[:half]
        send[:, at : at + chunk] = result[half:].astype(BF16)


def place_of(masks, member, shape, axis):
    block = iota(shape, axis) // CAP
    chip = jnp.zeros(shape, jnp.int32)
    for k, mask in enumerate(masks[: len(masks) // 2]):
        chip = jnp.where(block // EXPERTS == k, (member ^ mask) >> 1, chip)
    plane = (lax.axis_index("expert") // len(masks) + EXPERTS - block % EXPERTS) % EXPERTS
    return plane * (len(masks) // 2) + chip


def combine(masks, keep, came, flags, returned, chosen_out):
    chips = returned.shape[0]
    half, width = keep.shape
    group = len(masks)
    member = lax.axis_index("expert") % group
    total = keep[...] + came[...].astype(F32)
    for k, mask in enumerate(masks[: group // 2]):
        for z in range(EXPERTS):
            at = (k * EXPERTS + z) * CAP
            plane = lax.rem(lax.axis_index("expert") // group + EXPERTS - z, EXPERTS)
            chip = plane * (group // 2) + ((member ^ mask) >> 1)
            returned[chip, :, 0:width] = total[at : at + CAP].astype(BF16)
    rounded = total.astype(BF16)
    turns = chips // CAP
    place = place_of(masks, member, (half, ROWS), 0)
    wanted = iota((half, ROWS), 1) * turns
    span = (returned.shape[2] - width) // turns
    for r in range(turns):
        select = jnp.where(place == wanted + r, flags[0:half, 2:3], 0.0).astype(BF16)
        chosen = lax.dot_general(
            select, rounded, (((0,), (0,)), ((), ())), preferred_element_type=F32
        )[:CAP].astype(BF16)
        if span % LANES:
            chosen_out[r] = chosen
            continue
        columns = slice(width + r * span, width + (r + 1) * span)
        for q in range(chips):
            if q * span < width:
                returned[q, :, columns] = chosen[:, q * span : (q + 1) * span]
            else:
                returned[q, :, columns] = jnp.zeros((CAP, span), BF16)


def gather(width, came, out):
    chips = came.shape[0]
    turns = chips // CAP
    span = out.shape[1]
    total = came[0, :, width:].astype(F32)
    for q in range(1, chips):
        total = total + came[q, :, width:].astype(F32)
    for r in range(turns):
        out[r * CAP : (r + 1) * CAP, :] = total[:, r * span : (r + 1) * span]


def draft_fetch(masks, notes, fc, fc_out, early, sems):
    copy = pltpu.make_async_copy(fc.at[:, pl.ds(0, fc_out.shape[1])], fc_out, sems.at[0])
    copy.start()
    chips = early.shape[0] // 2
    half = notes.shape[0] // 2
    group = len(masks)
    me = lax.axis_index("expert")
    member, core = me % group, me % 2
    place = place_of(masks, member, (chips, half), 1)
    row = iota((chips, half), 0)
    wanted = (row % CAP) * (chips // CAP) + row // CAP
    select = jnp.logical_and(place == wanted, iota((chips, half), 1) % CAP == member)
    select = select.astype(F32).astype(BF16)
    same, other = [
        jnp.dot(
            select, notes[side * half : (side + 1) * half, :], preferred_element_type=F32
        )
        for side in range(2)
    ]
    early[0:chips, :] = jnp.where(core == 0, same, other)
    early[chips:, :] = jnp.where(core == 0, other, same)
    copy.wait()


def project(mine, other, early, fc_first, fc, out, rest, spread, sems):
    chips = mine.shape[0]
    devices, columns = early.shape
    pieces, step = out.shape[1:]
    ready = fc_first.shape[1] // step
    copies = [
        pltpu.make_async_copy(
            fc.at[:, pl.ds(i * step, step)], rest.at[i - ready], sems.at[i - ready]
        )
        for i in range(ready, pieces)
    ]
    for copy in copies:
        copy.start()
    core = lax.axis_index("expert") % 2
    sums = []
    for pair in ((mine, other), (other, mine)):
        total = jnp.where(core == 0, pair[0][...], pair[1][...])
        sums.append(jnp.where(core == 0, total[:, :columns], total[:, columns:]))
    inputs = (jnp.concatenate(sums, axis=0) + early[...]).astype(BF16)
    for i in range(pieces):
        if i < ready:
            block = fc_first[:, i * step : (i + 1) * step]
        else:
            copies[i - ready].wait()
            block = rest[i - ready]
        result = jnp.dot(inputs, block, preferred_element_type=F32)
        for k in range(step // LANES):
            spread[k, pl.ds(i, devices, stride=pieces), :] = result[
                :, k * LANES : (k + 1) * LANES
            ]
    turns = chips // CAP
    for c in range(2):
        for r in range(turns):
            for i in range(CAP):
                at = (c * chips + r * CAP + i) * pieces
                for k in range(step // LANES):
                    out[2 * (i * turns + r) + c, :, k * LANES : (k + 1) * LANES] = spread[
                        k, at : at + pieces, :
                    ].astype(BF16)


def finish(came, out):
    total = came[0].astype(F32)
    for d in range(1, came.shape[0]):
        total = total + came[d].astype(F32)
    step = total.shape[1]
    for i in range(total.shape[0]):
        out[:, i * step : (i + 1) * step] = total[i : i + 1].astype(BF16)


def settle(hidden, placing, came, out):
    chips = came.shape[0]
    width = out.shape[1]
    rows = jnp.concatenate(
        [came[q, :, 0:width].astype(F32) for q in range(chips)], axis=0
    ).astype(BF16)
    total = hidden[...] + jnp.dot(
        placing[...].astype(BF16), rows, preferred_element_type=F32
    )
    out[...] = total[: out.shape[0]].astype(BF16)


def far(array):
    return pltpu.with_memory_space_constraint(array, pltpu.HBM)


def near(array):
    return pltpu.with_memory_space_constraint(array, VMEM)


def early_of(notes, masks, devices, draft_rows):
    group, chips = len(masks), devices // 2
    member = lax.axis_index("expert") % group
    columns = notes.astype(F32).reshape(group, EXPERTS, group, draft_rows)
    columns = lax.dynamic_index_in_dim(columns, member, 2, keepdims=False)
    order = jnp.arange(devices)
    core, rest = order // chips, order % chips
    device = 2 * ((rest % CAP) * (chips // CAP) + rest // CAP) + core
    piece = jnp.zeros((group,), jnp.int32).at[jnp.array(masks)].set(jnp.arange(group))
    shift = (lax.axis_index("expert") // group - device // group) % EXPERTS
    return columns[piece[member ^ (device % group)], shift]


def params(mib):
    return pltpu.CompilerParams(vmem_limit_bytes=mib * MIB)


def per_device(
    queries,
    tree_key_value,
    key_value_cache,
    lengths,
    parents,
    residual,
    ffn_gain,
    router,
    routes,
    gate_weight,
    up_weight,
    down_weight,
    accepted,
    next_embed,
    draft_fc,
):
    devices = lax.axis_size("expert")
    chips = devices // 2
    group = devices // EXPERTS
    tokens, width = queries.shape
    assert lengths.shape[0] == 1 and tokens == TREE_NODES
    cache_slots, key_width = key_value_cache.shape[2:]
    hidden_units = gate_weight.shape[1]
    draft_rows = draft_fc.shape[0]
    ext = group * draft_rows // CAP
    total_width = width + ext + LANES
    same_core = [[2 * q + c for q in range(chips)] for c in range(2)]
    masks = [0]
    bits = [1 << i for i in range(group.bit_length() - 1)]
    for bit in reversed(bits):
        masks = masks + [mask | bit for mask in masks]

    def swap(array, bit):
        return lax.ppermute(array, "expert", [(d, d ^ bit) for d in range(devices)])

    first = 512 if hidden_units > 1024 else hidden_units // 2
    more = (256, 512) if hidden_units > 1024 else ()
    chunk = min(512, first)
    hidden, *parcels, placing, gate_first, up_first = pl.pallas_call(
        attend,
        out_shape=(
            jax.ShapeDtypeStruct((ROWS, width), F32),
            *[jax.ShapeDtypeStruct((CAP, total_width), BF16)] * EXPERTS,
            jax.ShapeDtypeStruct((ROWS, chips * CAP), F32),
            VMEM((width, first), BF16),
            VMEM((width, first), BF16),
        ),
        in_specs=[spec(SMEM)] * 2 + [spec(pl.ANY)] * 11,
        out_specs=(spec(VMEM),) * (4 + EXPERTS),
        scratch_shapes=[
            SMEM(parents.shape, jnp.int32),
            SMEM(routes.shape[::-1], jnp.int32),
            VMEM(queries.shape, BF16),
            VMEM(tree_key_value.shape, BF16),
            VMEM((cache_slots, key_width), BF16),
            VMEM((cache_slots, key_width), BF16),
            VMEM(residual.shape, BF16),
            VMEM((width // LANES, LANES), BF16),
            VMEM((EXPERTS, width), BF16),
            VMEM(next_embed.shape, BF16),
            VMEM((2, ROWS, key_width), F32),
            VMEM((ROWS, width), F32),
            VMEM((ROWS, width), F32),
            VMEM((EXPERTS, CAP, total_width), BF16),
            pltpu.SemaphoreType.DMA((12,)),
        ],
        compiler_params=params(12),
    )(
        lengths,
        accepted,
        far(parents),
        far(routes.T),
        far(queries),
        far(tree_key_value),
        far(key_value_cache),
        far(residual),
        far(ffn_gain.reshape(width // LANES, LANES)),
        far(router.T),
        far(next_embed),
        far(gate_weight),
        far(up_weight),
    )
    ready = [gate_first, up_first]

    def fetch_more(after, ready, more):
        at = sum(block.shape[1] for block in ready[::2])
        return ready + list(pl.pallas_call(
            functools.partial(fetch, at),
            out_shape=(VMEM((width, more), BF16), VMEM((width, more), BF16)),
            in_specs=[spec(pl.ANY)] * 3,
            out_specs=(spec(VMEM),) * 2,
            scratch_shapes=[pltpu.SemaphoreType.DMA((2,))],
            compiler_params=params(1),
            cost_estimate=pl.CostEstimate(
                flops=0, bytes_accessed=4 * width * more * 2, transcendentals=0
            ),
        )(after, far(gate_weight), far(up_weight)))

    for shift in range(1, EXPERTS):
        ring = [(d, (d + shift * group) % devices) for d in range(devices)]
        parcels[shift] = lax.ppermute(parcels[shift], "expert", ring)
    if more:
        ready = fetch_more(placing, ready, more[0])
        ready[-1], *parcels[1:] = lax.optimization_barrier((ready[-1], *parcels[1:]))
    pieces = [
        pl.pallas_call(
            join,
            out_shape=jax.ShapeDtypeStruct((EXPERTS, CAP, total_width), BF16),
            in_specs=[spec(VMEM)] * EXPERTS,
            out_specs=spec(VMEM),
            compiler_params=params(2),
        )(*parcels)
    ]
    for bit in reversed(bits[1:]):
        pieces = pieces + [swap(piece, bit) for piece in pieces]
    if more:
        ready = fetch_more(pieces[0], ready, more[1])
        ready[-1], *pieces[1:] = lax.optimization_barrier((ready[-1], *pieces[1:]))
    pieces = pieces + [swap(piece, 1) for piece in pieces]

    units = 8
    rows = 2 * chips * CAP
    padded_rows = -(-rows // 128) * 128
    keep, send, notes, weights = pl.pallas_call(
        functools.partial(experts, width, len(pieces), len(ready) // 2),
        out_shape=(
            VMEM((chips * CAP, width), F32),
            VMEM((chips * CAP, width), BF16),
            VMEM((rows, ext), BF16),
            VMEM((rows, LANES), F32),
        ),
        in_specs=[spec(VMEM)] * (len(pieces) + len(ready)) + [spec(pl.ANY)] * 3,
        out_specs=(spec(VMEM),) * 4,
        scratch_shapes=[
            VMEM((padded_rows, width), BF16),
            VMEM((padded_rows, hidden_units), BF16),
            VMEM((units, hidden_units, chunk), BF16),
            pltpu.SemaphoreType.DMA((units,)),
        ],
        compiler_params=params(21),
        cost_estimate=pl.CostEstimate(
            flops=2 * rows * width * hidden_units * 3,
            bytes_accessed=3 * down_weight.size * 2,
            transcendentals=0,
        ),
    )(
        *[near(piece) for piece in pieces],
        *[near(block) for block in ready],
        far(gate_weight),
        far(up_weight),
        far(down_weight),
    )
    came = swap(send, 1)
    fc_ready = width // 2
    fc_first, early = pl.pallas_call(
        functools.partial(draft_fetch, masks),
        out_shape=(
            VMEM((draft_rows, fc_ready), BF16),
            VMEM((devices, ext), F32),
        ),
        in_specs=[spec(VMEM), spec(pl.ANY)],
        out_specs=(spec(VMEM),) * 2,
        scratch_shapes=[pltpu.SemaphoreType.DMA((1,))],
        compiler_params=params(4),
        cost_estimate=pl.CostEstimate(
            flops=0, bytes_accessed=2 * draft_rows * fc_ready * 2, transcendentals=0
        ),
    )(near(notes), far(draft_fc))
    came, early = lax.optimization_barrier((came, early))
    span = 2 * draft_rows
    turns = chips // CAP
    partial, chosen = pl.pallas_call(
        functools.partial(combine, masks),
        out_shape=(
            jax.ShapeDtypeStruct((chips, CAP, width + turns * span), BF16),
            jax.ShapeDtypeStruct((turns, CAP, width if span % LANES else LANES), BF16),
        ),
        in_specs=[spec(VMEM)] * 3,
        out_specs=(spec(VMEM),) * 2,
        compiler_params=params(16),
    )(near(keep), came, near(weights))
    if span % LANES:
        chosen = chosen.reshape(turns, CAP, chips // 2, span).transpose(2, 1, 0, 3)
        chosen = chosen.reshape(chips // 2, CAP, turns * span)
        chosen = jnp.concatenate([chosen, jnp.zeros_like(chosen)], axis=0)
        partial = lax.dynamic_update_slice(partial, chosen, (0, 0, width))
    returned = lax.all_to_all(
        partial, "expert", 0, 0, tiled=True, axis_index_groups=same_core
    )
    if span % LANES:
        mine = jnp.sum(returned[:, :, width:].astype(F32), axis=0)
        mine = mine.reshape(CAP, turns, span).transpose(1, 0, 2).reshape(chips, span)
        early = early_of(notes, masks, devices, draft_rows)
    else:
        mine = pl.pallas_call(
            functools.partial(gather, width),
            out_shape=VMEM((chips, span), F32),
            in_specs=[spec(VMEM)],
            out_specs=spec(VMEM),
            compiler_params=params(4),
        )(returned)
    other = swap(mine, 1)
    sums = pl.pallas_call(
        project,
        out_shape=jax.ShapeDtypeStruct((devices, ROWS, width // ROWS), BF16),
        in_specs=[spec(VMEM)] * 4 + [spec(pl.ANY)],
        out_specs=spec(VMEM),
        scratch_shapes=[
            VMEM((ROWS - ROWS * fc_ready // width, draft_rows, width // ROWS), BF16),
            VMEM((width // ROWS // LANES, devices * ROWS, LANES), F32),
            pltpu.SemaphoreType.DMA((ROWS - ROWS * fc_ready // width,)),
        ],
        compiler_params=params(24),
    )(near(mine), other, near(early), near(fc_first), far(draft_fc))
    sums_came = lax.all_to_all(sums, "expert", 0, 0, tiled=True)
    layer_out = pl.pallas_call(
        settle,
        out_shape=jax.ShapeDtypeStruct((tokens, width), BF16),
        in_specs=[spec(VMEM)] * 3,
        out_specs=spec(VMEM),
        compiler_params=params(16),
    )(hidden, placing, returned)
    draft_out = pl.pallas_call(
        finish,
        out_shape=jax.ShapeDtypeStruct((1, width), BF16),
        in_specs=[spec(VMEM)],
        out_specs=spec(VMEM),
        compiler_params=params(8),
    )(sums_came)
    return (layer_out, draft_out)


def solution(mesh):
    return jax.shard_map(
        per_device,
        mesh=mesh,
        in_specs=(
            P(("groups", "expert"), None),
            P(("groups", "expert"), None, None),
            P(("groups", "expert"), None, None, None),
            P(("groups", "expert")),
            P(("groups", "expert")),
            P(("groups", "expert"), None),
            P(),
            P(),
            P(("groups", "expert"), None),
            P(None, "expert"),
            P(None, "expert"),
            P("expert", None),
            P(("groups", "expert")),
            P(("groups", "expert"), None),
            P("expert", None),
        ),
        out_specs=(P(("groups", "expert"), None), P(("groups", "expert"), None)),
        check_vma=False,
    )
```

```python
import functools
import jax
import jax.numpy as jnp
from jax import lax
from jax.experimental import pallas as pl
from jax.experimental.pallas import tpu as pltpu
from jax.sharding import PartitionSpec as P

QUERY_HEADS = 48
KEY_VALUE_HEADS = 8
HEAD_SIZE = 128
EXPERTS = 4
TREE_NODES = 6
CAP = 4
ROWS = 8
LANES = 128
EPSILON = 1e-05
HIDDEN = -1e30

F32 = jnp.float32
BF16 = jnp.bfloat16
VMEM = pltpu.VMEM
SMEM = pltpu.SMEM
MIB = 1 << 20


def spec(space):
    return pl.BlockSpec(memory_space=space)


def iota(shape, axis):
    return lax.broadcasted_iota(jnp.int32, shape, axis)


def along(values, shape, axis, fill=-1):
    index = iota(shape, axis)
    out = jnp.full(shape, fill, jnp.int32)
    for at, value in enumerate(values):
        out = jnp.where(index == at, value, out)
    return out


def attend(
    lengths,
    accepted,
    parents_far,
    routes_far,
    queries_far,
    tree_far,
    cache,
    residual_far,
    gain_far,
    router_far,
    embed_far,
    gate,
    up,
    hidden_out,
    send_0,
    send_1,
    send_2,
    send_3,
    placing_out,
    gate_first,
    up_first,
    parents,
    routes,
    queries,
    tree_key_value,
    keys,
    values,
    residual,
    gain,
    router,
    embed,
    tree,
    padded,
    hidden,
    payload,
    sems,
):
    width = queries.shape[1]
    per_expert = placing_out.shape[1] // (CAP * EXPERTS)
    draft_cols = payload.shape[2] - width - LANES
    shared = QUERY_HEADS // KEY_VALUE_HEADS
    first = gate_first.shape[1]
    moves = [
        (parents_far, parents),
        (routes_far, routes),
        (queries_far, queries),
        (tree_far, tree_key_value),
        (cache.at[0, 0], keys),
        (cache.at[0, 1], values),
        (residual_far, residual),
        (gain_far, gain),
        (router_far, router),
        (embed_far, embed),
        (gate.at[:, pl.ds(0, first)], gate_first),
        (up.at[:, pl.ds(0, first)], up_first),
    ]
    copies = [
        pltpu.make_async_copy(source, target, sems.at[i])
        for i, (source, target) in enumerate(moves)
    ]
    for copy in copies:
        copy.start()
    for copy in copies[:2]:
        copy.wait()

    bits = []
    for t in range(TREE_NODES):
        above = jnp.int32(0)
        for j in range(t):
            above = jnp.where(parents[t] == j, bits[j], above)
        bits.append(above | (1 << t))
    counts = [jnp.int32(0)] * EXPERTS
    slots = [[], []]
    for t in range(TREE_NODES):
        for k in range(2):
            slot = jnp.int32(0)
            for e in range(EXPERTS):
                slot = jnp.where(routes[k, t] == e, e * CAP + counts[e], slot)
            slots[k].append(slot)
        for e in range(EXPERTS):
            named = jnp.logical_or(routes[0, t] == e, routes[1, t] == e)
            counts[e] = counts[e] + named.astype(jnp.int32)

    tree[...] = jnp.zeros(tree.shape, F32)
    copies[2].wait()
    copies[3].wait()
    for t in range(TREE_NODES):
        pair = tree_key_value[t].astype(F32)
        tree[0, t : t + 1, :] = pair[0:1]
        tree[1, t : t + 1, :] = pair[1:2]
    padded[...] = jnp.zeros(padded.shape, F32)
    padded[0:TREE_NODES, :] = queries[...].astype(F32)

    slots_total = keys.shape[0]
    visible = iota((shared * ROWS, slots_total), 1) < lengths[0]
    row = iota((shared * ROWS, ROWS), 0) & (ROWS - 1)
    row_bits = jnp.ones((shared * ROWS, ROWS), jnp.int32)
    for t in range(TREE_NODES):
        row_bits = jnp.where(row == t, bits[t], row_bits)
    related = ((row_bits >> iota((shared * ROWS, ROWS), 1)) & 1) == 1
    scale = HEAD_SIZE ** (-0.5)
    contract_last = (((1,), (1,)), ((), ()))
    for copy in copies[4:10]:
        copy.wait()
    hidden[...] = jnp.zeros(hidden.shape, F32)
    hidden[0:TREE_NODES, :] = residual[...].astype(F32)
    for g in range(KEY_VALUE_HEADS):
        head = slice(g * HEAD_SIZE, (g + 1) * HEAD_SIZE)
        block = jnp.concatenate(
            [
                padded[:, (g * shared + i) * HEAD_SIZE : (g * shared + i + 1) * HEAD_SIZE]
                for i in range(shared)
            ],
            axis=0,
        ).astype(BF16)
        cache_scores = (
            lax.dot_general(block, keys[:, head], contract_last, preferred_element_type=F32)
            * scale
        )
        tree_scores = (
            lax.dot_general(
                block, tree[0, :, head].astype(BF16), contract_last, preferred_element_type=F32
            )
            * scale
        )
        cache_scores = jnp.where(visible, cache_scores, HIDDEN)
        tree_scores = jnp.where(related, tree_scores, HIDDEN)
        peak = jnp.maximum(
            jnp.max(cache_scores, axis=1, keepdims=True),
            jnp.max(tree_scores, axis=1, keepdims=True),
        )
        cache_exp = jnp.exp(cache_scores - peak)
        tree_exp = jnp.exp(tree_scores - peak)
        total = jnp.sum(cache_exp, axis=1, keepdims=True) + jnp.sum(
            tree_exp, axis=1, keepdims=True
        )
        share = 1.0 / total
        context = jnp.dot(
            (cache_exp * share).astype(BF16), values[:, head], preferred_element_type=F32
        ) + jnp.dot(
            (tree_exp * share).astype(BF16),
            tree[1, :, head].astype(BF16),
            preferred_element_type=F32,
        )
        for i in range(shared):
            columns = slice((g * shared + i) * HEAD_SIZE, (g * shared + i + 1) * HEAD_SIZE)
            hidden[:, columns] = hidden[:, columns] + context[i * ROWS : (i + 1) * ROWS]

    state = hidden[...]
    hidden_out[...] = state
    mean = jnp.sum(state * state, axis=1, keepdims=True) * (1.0 / width)
    gains = gain[...].astype(F32)
    shrink = lax.rsqrt(mean + EPSILON)
    normed = jnp.concatenate(
        [
            state[:, i * LANES : (i + 1) * LANES] * shrink * gains[i : i + 1]
            for i in range(width // LANES)
        ],
        axis=1,
    ).astype(BF16)
    logits = lax.dot_general(normed, router[...], contract_last, preferred_element_type=F32)
    expert = iota((ROWS, EXPERTS), 1)
    route = [
        along([routes[k, t] for t in range(TREE_NODES)], (ROWS, EXPERTS), 0) for k in range(2)
    ]
    picked_logit = [
        jnp.sum(jnp.where(expert == route[k], logits, 0.0), axis=1, keepdims=True)
        for k in range(2)
    ]
    first = jax.nn.sigmoid(picked_logit[0] - picked_logit[1])
    lane = iota((ROWS, LANES), 1)
    is_accepted = (iota((ROWS, LANES), 0) == accepted[0]).astype(F32)
    extras = []
    for weight in (first, 1.0 - first):
        high = weight.astype(BF16).astype(F32)
        extras.append(
            jnp.where(
                lane == 0,
                high,
                jnp.where(lane == 1, weight - high, jnp.where(lane == 2, is_accepted, 0.0)),
            ).astype(BF16)
        )
    place_row = iota((EXPERTS * ROWS, ROWS), 0)
    target = (place_row // ROWS) * CAP + (place_row & (ROWS - 1))
    target = jnp.where((place_row & (ROWS - 1)) < CAP, target, -2)
    hits = [
        (target == along(slots[k], (EXPERTS * ROWS, ROWS), 1)).astype(F32).astype(BF16)
        for k in range(2)
    ]
    packed = jnp.dot(hits[0] + hits[1], normed, preferred_element_type=F32)
    extra = jnp.dot(hits[0], extras[0], preferred_element_type=F32) + jnp.dot(
        hits[1], extras[1], preferred_element_type=F32
    )
    for e in range(EXPERTS):
        rows = packed[e * ROWS : e * ROWS + CAP].astype(BF16)
        last = extra[e * ROWS : e * ROWS + CAP].astype(BF16)
        payload[e, :, 0:width] = rows
        payload[e, :, width + draft_cols :] = last
    chosen = jnp.sum(
        jnp.where(iota((ROWS, width), 0) == accepted[0], state, 0.0), axis=0, keepdims=True
    )
    rest = embed[...].astype(F32)
    for e in range(EXPERTS):
        for i in range(CAP):
            at = (e * CAP + i) * draft_cols
            source = chosen if at < width else rest
            at = at % width
            payload[e, i : i + 1, width : width + draft_cols] = source[
                :, at : at + draft_cols
            ].astype(BF16)
    mine = lax.axis_index("expert") // (2 * per_expert)
    for shift, target in enumerate((send_0, send_1, send_2, send_3)):
        target[...] = payload[lax.rem(mine + shift, EXPERTS)]
    lane_slot = iota(placing_out.shape, 1)
    lane_slot = (lane_slot // (CAP * per_expert)) * CAP + lane_slot % CAP
    placing_out[...] = jnp.logical_or(
        lane_slot == along(slots[0], placing_out.shape, 0),
        lane_slot == along(slots[1], placing_out.shape, 0),
    ).astype(F32)
    for copy in copies[10:]:
        copy.wait()


def fetch(first, after, gate, up, gate_next, up_next, sems):
    del after
    columns = pl.ds(first, gate_next.shape[1])
    copies = [
        pltpu.make_async_copy(gate.at[:, columns], gate_next, sems.at[0]),
        pltpu.make_async_copy(up.at[:, columns], up_next, sems.at[1]),
    ]
    for copy in copies:
        copy.start()
    for copy in copies:
        copy.wait()


def join(*refs):
    for i, ref in enumerate(refs[:-1]):
        refs[-1][i] = ref[...]


def experts(width, sources, held, *refs):
    pieces, refs = refs[:sources], refs[sources:]
    ready, refs = refs[: 2 * held], refs[2 * held :]
    stream(width, pieces, ready, *refs)


def stream(
    width,
    pieces,
    ready,
    gate,
    up,
    down,
    keep,
    send,
    notes,
    weights,
    rows,
    acts,
    units,
    sems,
):
    whole_width = pieces[0].shape[2]
    half = keep.shape[0]
    count, depth, chunk = units.shape
    first = sum(block.shape[1] for block in ready[::2])
    parts = width // depth
    queue = []
    spans = [(at, min(chunk, depth - at)) for at in range(first, depth, chunk)]
    for at, span in spans:
        for source in (gate, up):
            for p in range(parts):
                queue.append((source.at[pl.ds(p * depth, depth), pl.ds(at, span)], span))
    for at in range(0, width, chunk):
        queue.append((down.at[:, pl.ds(at, chunk)], chunk))
    copies = [
        pltpu.make_async_copy(
            source, units.at[i % count, :, pl.ds(0, span)], sems.at[i % count]
        )
        for i, (source, span) in enumerate(queue)
    ]
    for copy in copies[:count]:
        copy.start()
    taken = 0

    def product(left):
        nonlocal taken
        copies[taken].wait()
        span = queue[taken][1]
        result = jnp.dot(
            left, units[taken % count, :, 0:span], preferred_element_type=F32
        )
        if taken + count < len(copies):
            copies[taken + count].start()
        taken += 1
        return result

    for k, source in enumerate(pieces):
        at = slice(k * EXPERTS * CAP, (k + 1) * EXPERTS * CAP)
        full = jnp.concatenate([source[z].astype(F32) for z in range(EXPERTS)], axis=0)
        rows[at, :] = full[:, 0:width].astype(BF16)
        notes[at, :] = full[:, width : whole_width - LANES].astype(BF16)
        weights[at, :] = full[:, whole_width - LANES :]
    if rows.shape[0] > 2 * half:
        rows[2 * half :, :] = jnp.zeros((rows.shape[0] - 2 * half, width), BF16)

    def activate(gate_val, up_val, at):
        acts[:, at : at + gate_val.shape[1]] = (
            gate_val / (1.0 + jnp.exp(-gate_val)) * up_val
        ).astype(BF16)

    base = 0
    for gate_block, up_block in zip(ready[::2], ready[1::2]):
        activate(
            jnp.dot(rows[...], gate_block[...], preferred_element_type=F32),
            jnp.dot(rows[...], up_block[...], preferred_element_type=F32),
            base,
        )
        base += gate_block.shape[1]
    for at, _ in spans:
        gate_val, up_val = [
            sum(product(rows[:, p * depth : (p + 1) * depth]) for p in range(parts))
            for _ in range(2)
        ]
        activate(gate_val, up_val, at)
    mix = weights[:, 0:1] + weights[:, 1:2]
    for at in range(0, width, chunk):
        result = product(acts[...])[: 2 * half] * mix
        keep[:, at : at + chunk] = result[:half]
        send[:, at : at + chunk] = result[half:].astype(BF16)


def place_of(masks, member, shape, axis):
    block = iota(shape, axis) // CAP
    chip = jnp.zeros(shape, jnp.int32)
    for k, mask in enumerate(masks[: len(masks) // 2]):
        chip = jnp.where(block // EXPERTS == k, (member ^ mask) >> 1, chip)
    plane = (lax.axis_index("expert") // len(masks) + EXPERTS - block % EXPERTS) % EXPERTS
    return plane * (len(masks) // 2) + chip


def combine(masks, keep, came, flags, returned, chosen_out):
    chips = returned.shape[0]
    half, width = keep.shape
    group = len(masks)
    member = lax.axis_index("expert") % group
    total = keep[...] + came[...].astype(F32)
    for k, mask in enumerate(masks[: group // 2]):
        for z in range(EXPERTS):
            at = (k * EXPERTS + z) * CAP
            plane = lax.rem(lax.axis_index("expert") // group + EXPERTS - z, EXPERTS)
            chip = plane * (group // 2) + ((member ^ mask) >> 1)
            returned[chip, :, 0:width] = total[at : at + CAP].astype(BF16)
    rounded = total.astype(BF16)
    turns = chips // CAP
    place = place_of(masks, member, (half, ROWS), 0)
    wanted = iota((half, ROWS), 1) * turns
    span = (returned.shape[2] - width) // turns
    for r in range(turns):
        select = jnp.where(place == wanted + r, flags[0:half, 2:3], 0.0).astype(BF16)
        chosen = lax.dot_general(
            select, rounded, (((0,), (0,)), ((), ())), preferred_element_type=F32
        )[:CAP].astype(BF16)
        if span % LANES:
            chosen_out[r] = chosen
            continue
        columns = slice(width + r * span, width + (r + 1) * span)
        for q in range(chips):
            if q * span < width:
                returned[q, :, columns] = chosen[:, q * span : (q + 1) * span]
            else:
                returned[q, :, columns] = jnp.zeros((CAP, span), BF16)


def gather(width, came, out):
    chips = came.shape[0]
    turns = chips // CAP
    span = out.shape[1]
    total = came[0, :, width:].astype(F32)
    for q in range(1, chips):
        total = total + came[q, :, width:].astype(F32)
    for r in range(turns):
        out[r * CAP : (r + 1) * CAP, :] = total[:, r * span : (r + 1) * span]


def draft_fetch(masks, notes, fc, fc_out, early, sems):
    copy = pltpu.make_async_copy(fc.at[:, pl.ds(0, fc_out.shape[1])], fc_out, sems.at[0])
    copy.start()
    chips = early.shape[0] // 2
    half = notes.shape[0] // 2
    group = len(masks)
    me = lax.axis_index("expert")
    member, core = me % group, me % 2
    place = place_of(masks, member, (chips, half), 1)
    row = iota((chips, half), 0)
    wanted = (row % CAP) * (chips // CAP) + row // CAP
    select = jnp.logical_and(place == wanted, iota((chips, half), 1) % CAP == member)
    select = select.astype(F32).astype(BF16)
    same, other = [
        jnp.dot(
            select, notes[side * half : (side + 1) * half, :], preferred_element_type=F32
        )
        for side in range(2)
    ]
    early[0:chips, :] = jnp.where(core == 0, same, other)
    early[chips:, :] = jnp.where(core == 0, other, same)
    copy.wait()


def project(mine, other, early, fc_first, fc, out, rest, spread, sems):
    chips = mine.shape[0]
    devices, columns = early.shape
    pieces, step = out.shape[1:]
    ready = fc_first.shape[1] // step
    copies = [
        pltpu.make_async_copy(
            fc.at[:, pl.ds(i * step, step)], rest.at[i - ready], sems.at[i - ready]
        )
        for i in range(ready, pieces)
    ]
    for copy in copies:
        copy.start()
    core = lax.axis_index("expert") % 2
    sums = []
    for pair in ((mine, other), (other, mine)):
        total = jnp.where(core == 0, pair[0][...], pair[1][...])
        sums.append(jnp.where(core == 0, total[:, :columns], total[:, columns:]))
    inputs = (jnp.concatenate(sums, axis=0) + early[...]).astype(BF16)
    for i in range(pieces):
        if i < ready:
            block = fc_first[:, i * step : (i + 1) * step]
        else:
            copies[i - ready].wait()
            block = rest[i - ready]
        result = jnp.dot(inputs, block, preferred_element_type=F32)
        for k in range(step // LANES):
            spread[k, pl.ds(i, devices, stride=pieces), :] = result[
                :, k * LANES : (k + 1) * LANES
            ]
    turns = chips // CAP
    for c in range(2):
        for r in range(turns):
            for i in range(CAP):
                at = (c * chips + r * CAP + i) * pieces
                for k in range(step // LANES):
                    out[2 * (i * turns + r) + c, :, k * LANES : (k + 1) * LANES] = spread[
                        k, at : at + pieces, :
                    ].astype(BF16)


def finish(came, out):
    total = came[0].astype(F32)
    for d in range(1, came.shape[0]):
        total = total + came[d].astype(F32)
    step = total.shape[1]
    for i in range(total.shape[0]):
        out[:, i * step : (i + 1) * step] = total[i : i + 1].astype(BF16)


def settle(hidden, placing, came, out):
    chips = came.shape[0]
    width = out.shape[1]
    rows = jnp.concatenate(
        [came[q, :, 0:width].astype(F32) for q in range(chips)], axis=0
    ).astype(BF16)
    total = hidden[...] + jnp.dot(
        placing[...].astype(BF16), rows, preferred_element_type=F32
    )
    out[...] = total[: out.shape[0]].astype(BF16)


def far(array):
    return pltpu.with_memory_space_constraint(array, pltpu.HBM)


def near(array):
    return pltpu.with_memory_space_constraint(array, VMEM)


def early_of(notes, masks, devices, draft_rows):
    group, chips = len(masks), devices // 2
    member = lax.axis_index("expert") % group
    columns = notes.astype(F32).reshape(group, EXPERTS, group, draft_rows)
    columns = lax.dynamic_index_in_dim(columns, member, 2, keepdims=False)
    order = jnp.arange(devices)
    core, rest = order // chips, order % chips
    device = 2 * ((rest % CAP) * (chips // CAP) + rest // CAP) + core
    piece = jnp.zeros((group,), jnp.int32).at[jnp.array(masks)].set(jnp.arange(group))
    shift = (lax.axis_index("expert") // group - device // group) % EXPERTS
    return columns[piece[member ^ (device % group)], shift]


def params(mib):
    return pltpu.CompilerParams(vmem_limit_bytes=mib * MIB)


def per_device(
    queries,
    tree_key_value,
    key_value_cache,
    lengths,
    parents,
    residual,
    ffn_gain,
    router,
    routes,
    gate_weight,
    up_weight,
    down_weight,
    accepted,
    next_embed,
    draft_fc,
):
    devices = lax.axis_size("expert")
    chips = devices // 2
    group = devices // EXPERTS
    tokens, width = queries.shape
    assert lengths.shape[0] == 1 and tokens == TREE_NODES
    cache_slots, key_width = key_value_cache.shape[2:]
    hidden_units = gate_weight.shape[1]
    draft_rows = draft_fc.shape[0]
    ext = group * draft_rows // CAP
    total_width = width + ext + LANES
    same_core = [[2 * q + c for q in range(chips)] for c in range(2)]
    masks = [0]
    bits = [1 << i for i in range(group.bit_length() - 1)]
    for bit in reversed(bits):
        masks = masks + [mask | bit for mask in masks]

    def swap(array, bit):
        return lax.ppermute(array, "expert", [(d, d ^ bit) for d in range(devices)])

    first = 512 if hidden_units > 1024 else hidden_units // 2
    more = (256, 512) if hidden_units > 1024 else ()
    chunk = min(512, first)
    hidden, *parcels, placing, gate_first, up_first = pl.pallas_call(
        attend,
        out_shape=(
            jax.ShapeDtypeStruct((ROWS, width), F32),
            *[jax.ShapeDtypeStruct((CAP, total_width), BF16)] * EXPERTS,
            jax.ShapeDtypeStruct((ROWS, chips * CAP), F32),
            VMEM((width, first), BF16),
            VMEM((width, first), BF16),
        ),
        in_specs=[spec(SMEM)] * 2 + [spec(pl.ANY)] * 11,
        out_specs=(spec(VMEM),) * (4 + EXPERTS),
        scratch_shapes=[
            SMEM(parents.shape, jnp.int32),
            SMEM(routes.shape[::-1], jnp.int32),
            VMEM(queries.shape, BF16),
            VMEM(tree_key_value.shape, BF16),
            VMEM((cache_slots, key_width), BF16),
            VMEM((cache_slots, key_width), BF16),
            VMEM(residual.shape, BF16),
            VMEM((width // LANES, LANES), BF16),
            VMEM((EXPERTS, width), BF16),
            VMEM(next_embed.shape, BF16),
            VMEM((2, ROWS, key_width), F32),
            VMEM((ROWS, width), F32),
            VMEM((ROWS, width), F32),
            VMEM((EXPERTS, CAP, total_width), BF16),
            pltpu.SemaphoreType.DMA((12,)),
        ],
        compiler_params=params(12),
    )(
        lengths,
        accepted,
        far(parents),
        far(routes.T),
        far(queries),
        far(tree_key_value),
        far(key_value_cache),
        far(residual),
        far(ffn_gain.reshape(width // LANES, LANES)),
        far(router.T),
        far(next_embed),
        far(gate_weight),
        far(up_weight),
    )
    ready = [gate_first, up_first]

    def fetch_more(after, ready, more):
        at = sum(block.shape[1] for block in ready[::2])
        return ready + list(pl.pallas_call(
            functools.partial(fetch, at),
            out_shape=(VMEM((width, more), BF16), VMEM((width, more), BF16)),
            in_specs=[spec(pl.ANY)] * 3,
            out_specs=(spec(VMEM),) * 2,
            scratch_shapes=[pltpu.SemaphoreType.DMA((2,))],
            compiler_params=params(1),
            cost_estimate=pl.CostEstimate(
                flops=0, bytes_accessed=4 * width * more * 2, transcendentals=0
            ),
        )(after, far(gate_weight), far(up_weight)))

    for shift in range(1, EXPERTS):
        ring = [(d, (d + shift * group) % devices) for d in range(devices)]
        parcels[shift] = lax.ppermute(parcels[shift], "expert", ring)
    if more:
        ready = fetch_more(placing, ready, more[0])
        ready[-1], *parcels[1:] = lax.optimization_barrier((ready[-1], *parcels[1:]))
    pieces = [
        pl.pallas_call(
            join,
            out_shape=jax.ShapeDtypeStruct((EXPERTS, CAP, total_width), BF16),
            in_specs=[spec(VMEM)] * EXPERTS,
            out_specs=spec(VMEM),
            compiler_params=params(2),
        )(*parcels)
    ]
    for bit in reversed(bits[1:]):
        pieces = pieces + [swap(piece, bit) for piece in pieces]
    if more:
        ready = fetch_more(pieces[0], ready, more[1])
        ready[-1], *pieces[1:] = lax.optimization_barrier((ready[-1], *pieces[1:]))
    pieces = pieces + [swap(piece, 1) for piece in pieces]

    units = 10
    rows = 2 * chips * CAP
    padded_rows = -(-rows // 128) * 128
    keep, send, notes, weights = pl.pallas_call(
        functools.partial(experts, width, len(pieces), len(ready) // 2),
        out_shape=(
            VMEM((chips * CAP, width), F32),
            VMEM((chips * CAP, width), BF16),
            VMEM((rows, ext), BF16),
            VMEM((rows, LANES), F32),
        ),
        in_specs=[spec(VMEM)] * (len(pieces) + len(ready)) + [spec(pl.ANY)] * 3,
        out_specs=(spec(VMEM),) * 4,
        scratch_shapes=[
            VMEM((padded_rows, width), BF16),
            VMEM((padded_rows, hidden_units), BF16),
            VMEM((units, hidden_units, chunk), BF16),
            pltpu.SemaphoreType.DMA((units,)),
        ],
        compiler_params=params(25),
        cost_estimate=pl.CostEstimate(
            flops=2 * rows * width * hidden_units * 3,
            bytes_accessed=3 * down_weight.size * 2,
            transcendentals=0,
        ),
    )(
        *[near(piece) for piece in pieces],
        *[near(block) for block in ready],
        far(gate_weight),
        far(up_weight),
        far(down_weight),
    )
    came = swap(send, 1)
    fc_ready = width // 2
    fc_first, early = pl.pallas_call(
        functools.partial(draft_fetch, masks),
        out_shape=(
            VMEM((draft_rows, fc_ready), BF16),
            VMEM((devices, ext), F32),
        ),
        in_specs=[spec(VMEM), spec(pl.ANY)],
        out_specs=(spec(VMEM),) * 2,
        scratch_shapes=[pltpu.SemaphoreType.DMA((1,))],
        compiler_params=params(4),
        cost_estimate=pl.CostEstimate(
            flops=0, bytes_accessed=2 * draft_rows * fc_ready * 2, transcendentals=0
        ),
    )(near(notes), far(draft_fc))
    came, early = lax.optimization_barrier((came, early))
    span = 2 * draft_rows
    turns = chips // CAP
    partial, chosen = pl.pallas_call(
        functools.partial(combine, masks),
        out_shape=(
            jax.ShapeDtypeStruct((chips, CAP, width + turns * span), BF16),
            jax.ShapeDtypeStruct((turns, CAP, width if span % LANES else LANES), BF16),
        ),
        in_specs=[spec(VMEM)] * 3,
        out_specs=(spec(VMEM),) * 2,
        compiler_params=params(16),
    )(near(keep), came, near(weights))
    if span % LANES:
        chosen = chosen.reshape(turns, CAP, chips // 2, span).transpose(2, 1, 0, 3)
        chosen = chosen.reshape(chips // 2, CAP, turns * span)
        chosen = jnp.concatenate([chosen, jnp.zeros_like(chosen)], axis=0)
        partial = lax.dynamic_update_slice(partial, chosen, (0, 0, width))
    returned = lax.all_to_all(
        partial, "expert", 0, 0, tiled=True, axis_index_groups=same_core
    )
    if span % LANES:
        mine = jnp.sum(returned[:, :, width:].astype(F32), axis=0)
        mine = mine.reshape(CAP, turns, span).transpose(1, 0, 2).reshape(chips, span)
        early = early_of(notes, masks, devices, draft_rows)
    else:
        mine = pl.pallas_call(
            functools.partial(gather, width),
            out_shape=VMEM((chips, span), F32),
            in_specs=[spec(VMEM)],
            out_specs=spec(VMEM),
            compiler_params=params(4),
        )(returned)
    other = swap(mine, 1)
    sums = pl.pallas_call(
        project,
        out_shape=jax.ShapeDtypeStruct((devices, ROWS, width // ROWS), BF16),
        in_specs=[spec(VMEM)] * 4 + [spec(pl.ANY)],
        out_specs=spec(VMEM),
        scratch_shapes=[
            VMEM((ROWS - ROWS * fc_ready // width, draft_rows, width // ROWS), BF16),
            VMEM((width // ROWS // LANES, devices * ROWS, LANES), F32),
            pltpu.SemaphoreType.DMA((ROWS - ROWS * fc_ready // width,)),
        ],
        compiler_params=params(24),
    )(near(mine), other, near(early), near(fc_first), far(draft_fc))
    sums_came = lax.all_to_all(sums, "expert", 0, 0, tiled=True)
    layer_out = pl.pallas_call(
        settle,
        out_shape=jax.ShapeDtypeStruct((tokens, width), BF16),
        in_specs=[spec(VMEM)] * 3,
        out_specs=spec(VMEM),
        compiler_params=params(16),
    )(hidden, placing, returned)
    draft_out = pl.pallas_call(
        finish,
        out_shape=jax.ShapeDtypeStruct((1, width), BF16),
        in_specs=[spec(VMEM)],
        out_specs=spec(VMEM),
        compiler_params=params(8),
    )(sums_came)
    return (layer_out, draft_out)


def solution(mesh):
    return jax.shard_map(
        per_device,
        mesh=mesh,
        in_specs=(
            P(("groups", "expert"), None),
            P(("groups", "expert"), None, None),
            P(("groups", "expert"), None, None, None),
            P(("groups", "expert")),
            P(("groups", "expert")),
            P(("groups", "expert"), None),
            P(),
            P(),
            P(("groups", "expert"), None),
            P(None, "expert"),
            P(None, "expert"),
            P("expert", None),
            P(("groups", "expert")),
            P(("groups", "expert"), None),
            P("expert", None),
        ),
        out_specs=(P(("groups", "expert"), None), P(("groups", "expert"), None)),
        check_vma=False,
    )
```

```python
import functools
import jax
import jax.numpy as jnp
from jax import lax
from jax.experimental import pallas as pl
from jax.experimental.pallas import tpu as pltpu
from jax.sharding import PartitionSpec as P

QUERY_HEADS = 48
KEY_VALUE_HEADS = 8
HEAD_SIZE = 128
EXPERTS = 4
TREE_NODES = 6
CAP = 4
ROWS = 8
LANES = 128
EPSILON = 1e-05
HIDDEN = -1e30

F32 = jnp.float32
BF16 = jnp.bfloat16
VMEM = pltpu.VMEM
SMEM = pltpu.SMEM
MIB = 1 << 20


def spec(space):
    return pl.BlockSpec(memory_space=space)


def iota(shape, axis):
    return lax.broadcasted_iota(jnp.int32, shape, axis)


def along(values, shape, axis, fill=-1):
    index = iota(shape, axis)
    out = jnp.full(shape, fill, jnp.int32)
    for at, value in enumerate(values):
        out = jnp.where(index == at, value, out)
    return out


def attend(
    lengths,
    accepted,
    parents_far,
    routes_far,
    queries_far,
    tree_far,
    cache,
    residual_far,
    gain_far,
    router_far,
    embed_far,
    gate,
    up,
    hidden_out,
    send_0,
    send_1,
    send_2,
    send_3,
    placing_out,
    gate_first,
    up_first,
    parents,
    routes,
    queries,
    tree_key_value,
    keys,
    values,
    residual,
    gain,
    router,
    embed,
    tree,
    padded,
    hidden,
    payload,
    sems,
):
    width = queries.shape[1]
    per_expert = placing_out.shape[1] // (CAP * EXPERTS)
    draft_cols = payload.shape[2] - width - LANES
    shared = QUERY_HEADS // KEY_VALUE_HEADS
    first = gate_first.shape[1]
    moves = [
        (parents_far, parents),
        (routes_far, routes),
        (queries_far, queries),
        (tree_far, tree_key_value),
        (cache.at[0, 0], keys),
        (cache.at[0, 1], values),
        (residual_far, residual),
        (gain_far, gain),
        (router_far, router),
        (embed_far, embed),
        (gate.at[:, pl.ds(0, first)], gate_first),
        (up.at[:, pl.ds(0, first)], up_first),
    ]
    copies = [
        pltpu.make_async_copy(source, target, sems.at[i])
        for i, (source, target) in enumerate(moves)
    ]
    for copy in copies:
        copy.start()
    for copy in copies[:2]:
        copy.wait()

    bits = []
    for t in range(TREE_NODES):
        above = jnp.int32(0)
        for j in range(t):
            above = jnp.where(parents[t] == j, bits[j], above)
        bits.append(above | (1 << t))
    counts = [jnp.int32(0)] * EXPERTS
    slots = [[], []]
    for t in range(TREE_NODES):
        for k in range(2):
            slot = jnp.int32(0)
            for e in range(EXPERTS):
                slot = jnp.where(routes[k, t] == e, e * CAP + counts[e], slot)
            slots[k].append(slot)
        for e in range(EXPERTS):
            named = jnp.logical_or(routes[0, t] == e, routes[1, t] == e)
            counts[e] = counts[e] + named.astype(jnp.int32)

    tree[...] = jnp.zeros(tree.shape, F32)
    copies[2].wait()
    copies[3].wait()
    for t in range(TREE_NODES):
        pair = tree_key_value[t].astype(F32)
        tree[0, t : t + 1, :] = pair[0:1]
        tree[1, t : t + 1, :] = pair[1:2]
    padded[...] = jnp.zeros(padded.shape, F32)
    padded[0:TREE_NODES, :] = queries[...].astype(F32)

    slots_total = keys.shape[0]
    visible = iota((shared * ROWS, slots_total), 1) < lengths[0]
    row = iota((shared * ROWS, ROWS), 0) & (ROWS - 1)
    row_bits = jnp.ones((shared * ROWS, ROWS), jnp.int32)
    for t in range(TREE_NODES):
        row_bits = jnp.where(row == t, bits[t], row_bits)
    related = ((row_bits >> iota((shared * ROWS, ROWS), 1)) & 1) == 1
    scale = HEAD_SIZE ** (-0.5)
    contract_last = (((1,), (1,)), ((), ()))
    for copy in copies[4:10]:
        copy.wait()
    hidden[...] = jnp.zeros(hidden.shape, F32)
    hidden[0:TREE_NODES, :] = residual[...].astype(F32)
    for g in range(KEY_VALUE_HEADS):
        head = slice(g * HEAD_SIZE, (g + 1) * HEAD_SIZE)
        block = jnp.concatenate(
            [
                padded[:, (g * shared + i) * HEAD_SIZE : (g * shared + i + 1) * HEAD_SIZE]
                for i in range(shared)
            ],
            axis=0,
        ).astype(BF16)
        cache_scores = (
            lax.dot_general(block, keys[:, head], contract_last, preferred_element_type=F32)
            * scale
        )
        tree_scores = (
            lax.dot_general(
                block, tree[0, :, head].astype(BF16), contract_last, preferred_element_type=F32
            )
            * scale
        )
        cache_scores = jnp.where(visible, cache_scores, HIDDEN)
        tree_scores = jnp.where(related, tree_scores, HIDDEN)
        peak = jnp.maximum(
            jnp.max(cache_scores, axis=1, keepdims=True),
            jnp.max(tree_scores, axis=1, keepdims=True),
        )
        cache_exp = jnp.exp(cache_scores - peak)
        tree_exp = jnp.exp(tree_scores - peak)
        total = jnp.sum(cache_exp, axis=1, keepdims=True) + jnp.sum(
            tree_exp, axis=1, keepdims=True
        )
        share = 1.0 / total
        context = jnp.dot(
            (cache_exp * share).astype(BF16), values[:, head], preferred_element_type=F32
        ) + jnp.dot(
            (tree_exp * share).astype(BF16),
            tree[1, :, head].astype(BF16),
            preferred_element_type=F32,
        )
        for i in range(shared):
            columns = slice((g * shared + i) * HEAD_SIZE, (g * shared + i + 1) * HEAD_SIZE)
            hidden[:, columns] = hidden[:, columns] + context[i * ROWS : (i + 1) * ROWS]

    state = hidden[...]
    hidden_out[...] = state
    mean = jnp.sum(state * state, axis=1, keepdims=True) * (1.0 / width)
    gains = gain[...].astype(F32)
    shrink = lax.rsqrt(mean + EPSILON)
    normed = jnp.concatenate(
        [
            state[:, i * LANES : (i + 1) * LANES] * shrink * gains[i : i + 1]
            for i in range(width // LANES)
        ],
        axis=1,
    ).astype(BF16)
    logits = lax.dot_general(normed, router[...], contract_last, preferred_element_type=F32)
    expert = iota((ROWS, EXPERTS), 1)
    route = [
        along([routes[k, t] for t in range(TREE_NODES)], (ROWS, EXPERTS), 0) for k in range(2)
    ]
    picked_logit = [
        jnp.sum(jnp.where(expert == route[k], logits, 0.0), axis=1, keepdims=True)
        for k in range(2)
    ]
    first = jax.nn.sigmoid(picked_logit[0] - picked_logit[1])
    lane = iota((ROWS, LANES), 1)
    is_accepted = (iota((ROWS, LANES), 0) == accepted[0]).astype(F32)
    extras = []
    for weight in (first, 1.0 - first):
        high = weight.astype(BF16).astype(F32)
        extras.append(
            jnp.where(
                lane == 0,
                high,
                jnp.where(lane == 1, weight - high, jnp.where(lane == 2, is_accepted, 0.0)),
            ).astype(BF16)
        )
    place_row = iota((EXPERTS * ROWS, ROWS), 0)
    target = (place_row // ROWS) * CAP + (place_row & (ROWS - 1))
    target = jnp.where((place_row & (ROWS - 1)) < CAP, target, -2)
    hits = [
        (target == along(slots[k], (EXPERTS * ROWS, ROWS), 1)).astype(F32).astype(BF16)
        for k in range(2)
    ]
    packed = jnp.dot(hits[0] + hits[1], normed, preferred_element_type=F32)
    extra = jnp.dot(hits[0], extras[0], preferred_element_type=F32) + jnp.dot(
        hits[1], extras[1], preferred_element_type=F32
    )
    for e in range(EXPERTS):
        rows = packed[e * ROWS : e * ROWS + CAP].astype(BF16)
        last = extra[e * ROWS : e * ROWS + CAP].astype(BF16)
        payload[e, :, 0:width] = rows
        payload[e, :, width + draft_cols :] = last
    chosen = jnp.sum(
        jnp.where(iota((ROWS, width), 0) == accepted[0], state, 0.0), axis=0, keepdims=True
    )
    rest = embed[...].astype(F32)
    for e in range(EXPERTS):
        for i in range(CAP):
            at = (e * CAP + i) * draft_cols
            source = chosen if at < width else rest
            at = at % width
            payload[e, i : i + 1, width : width + draft_cols] = source[
                :, at : at + draft_cols
            ].astype(BF16)
    mine = lax.axis_index("expert") // (2 * per_expert)
    for shift, target in enumerate((send_0, send_1, send_2, send_3)):
        target[...] = payload[lax.rem(mine + shift, EXPERTS)]
    lane_slot = iota(placing_out.shape, 1)
    lane_slot = (lane_slot // (CAP * per_expert)) * CAP + lane_slot % CAP
    placing_out[...] = jnp.logical_or(
        lane_slot == along(slots[0], placing_out.shape, 0),
        lane_slot == along(slots[1], placing_out.shape, 0),
    ).astype(F32)
    for copy in copies[10:]:
        copy.wait()


def fetch(first, after, gate, up, gate_next, up_next, sems):
    del after
    columns = pl.ds(first, gate_next.shape[1])
    copies = [
        pltpu.make_async_copy(gate.at[:, columns], gate_next, sems.at[0]),
        pltpu.make_async_copy(up.at[:, columns], up_next, sems.at[1]),
    ]
    for copy in copies:
        copy.start()
    for copy in copies:
        copy.wait()


def join(*refs):
    for i, ref in enumerate(refs[:-1]):
        refs[-1][i] = ref[...]


def experts(width, sources, held, *refs):
    pieces, refs = refs[:sources], refs[sources:]
    ready, refs = refs[: 2 * held], refs[2 * held :]
    stream(width, pieces, ready, *refs)


def stream(
    width,
    pieces,
    ready,
    gate,
    up,
    down,
    keep,
    send,
    notes,
    weights,
    rows,
    acts,
    units,
    sems,
):
    whole_width = pieces[0].shape[2]
    half = keep.shape[0]
    count, depth, chunk = units.shape
    first = sum(block.shape[1] for block in ready[::2])
    parts = width // depth
    queue = []
    spans = [(at, min(chunk, depth - at)) for at in range(first, depth, chunk)]
    for at, span in spans:
        for source in (gate, up):
            for p in range(parts):
                queue.append((source.at[pl.ds(p * depth, depth), pl.ds(at, span)], span))
    for at in range(0, width, chunk):
        queue.append((down.at[:, pl.ds(at, chunk)], chunk))
    copies = [
        pltpu.make_async_copy(
            source, units.at[i % count, :, pl.ds(0, span)], sems.at[i % count]
        )
        for i, (source, span) in enumerate(queue)
    ]
    for copy in copies[:count]:
        copy.start()
    taken = 0

    def product(left):
        nonlocal taken
        copies[taken].wait()
        span = queue[taken][1]
        result = jnp.dot(
            left, units[taken % count, :, 0:span], preferred_element_type=F32
        )
        if taken + count < len(copies):
            copies[taken + count].start()
        taken += 1
        return result

    for k, source in enumerate(pieces):
        at = slice(k * EXPERTS * CAP, (k + 1) * EXPERTS * CAP)
        full = jnp.concatenate([source[z].astype(F32) for z in range(EXPERTS)], axis=0)
        rows[at, :] = full[:, 0:width].astype(BF16)
        notes[at, :] = full[:, width : whole_width - LANES].astype(BF16)
        weights[at, :] = full[:, whole_width - LANES :]
    if rows.shape[0] > 2 * half:
        rows[2 * half :, :] = jnp.zeros((rows.shape[0] - 2 * half, width), BF16)

    def activate(gate_val, up_val, at):
        acts[:, at : at + gate_val.shape[1]] = (
            gate_val / (1.0 + jnp.exp(-gate_val)) * up_val
        ).astype(BF16)

    base = 0
    for gate_block, up_block in zip(ready[::2], ready[1::2]):
        activate(
            jnp.dot(rows[...], gate_block[...], preferred_element_type=F32),
            jnp.dot(rows[...], up_block[...], preferred_element_type=F32),
            base,
        )
        base += gate_block.shape[1]
    for at, _ in spans:
        gate_val, up_val = [
            sum(product(rows[:, p * depth : (p + 1) * depth]) for p in range(parts))
            for _ in range(2)
        ]
        activate(gate_val, up_val, at)
    mix = weights[:, 0:1] + weights[:, 1:2]
    for at in range(0, width, chunk):
        result = product(acts[...])[: 2 * half] * mix
        keep[:, at : at + chunk] = result[:half]
        send[:, at : at + chunk] = result[half:].astype(BF16)


def place_of(masks, member, shape, axis):
    block = iota(shape, axis) // CAP
    chip = jnp.zeros(shape, jnp.int32)
    for k, mask in enumerate(masks[: len(masks) // 2]):
        chip = jnp.where(block // EXPERTS == k, (member ^ mask) >> 1, chip)
    plane = (lax.axis_index("expert") // len(masks) + EXPERTS - block % EXPERTS) % EXPERTS
    return plane * (len(masks) // 2) + chip


def combine(masks, keep, came, flags, returned, chosen_out):
    chips = returned.shape[0]
    half, width = keep.shape
    group = len(masks)
    member = lax.axis_index("expert") % group
    total = keep[...] + came[...].astype(F32)
    for k, mask in enumerate(masks[: group // 2]):
        for z in range(EXPERTS):
            at = (k * EXPERTS + z) * CAP
            plane = lax.rem(lax.axis_index("expert") // group + EXPERTS - z, EXPERTS)
            chip = plane * (group // 2) + ((member ^ mask) >> 1)
            returned[chip, :, 0:width] = total[at : at + CAP].astype(BF16)
    rounded = total.astype(BF16)
    turns = chips // CAP
    place = place_of(masks, member, (half, ROWS), 0)
    wanted = iota((half, ROWS), 1) * turns
    span = (returned.shape[2] - width) // turns
    for r in range(turns):
        select = jnp.where(place == wanted + r, flags[0:half, 2:3], 0.0).astype(BF16)
        chosen = lax.dot_general(
            select, rounded, (((0,), (0,)), ((), ())), preferred_element_type=F32
        )[:CAP].astype(BF16)
        if span % LANES:
            chosen_out[r] = chosen
            continue
        columns = slice(width + r * span, width + (r + 1) * span)
        for q in range(chips):
            if q * span < width:
                returned[q, :, columns] = chosen[:, q * span : (q + 1) * span]
            else:
                returned[q, :, columns] = jnp.zeros((CAP, span), BF16)


def gather(width, came, out):
    chips = came.shape[0]
    turns = chips // CAP
    span = out.shape[1]
    total = came[0, :, width:].astype(F32)
    for q in range(1, chips):
        total = total + came[q, :, width:].astype(F32)
    for r in range(turns):
        out[r * CAP : (r + 1) * CAP, :] = total[:, r * span : (r + 1) * span]


def draft_fetch(masks, notes, fc, fc_out, early, sems):
    copy = pltpu.make_async_copy(fc.at[:, pl.ds(0, fc_out.shape[1])], fc_out, sems.at[0])
    copy.start()
    chips = early.shape[0] // 2
    half = notes.shape[0] // 2
    group = len(masks)
    me = lax.axis_index("expert")
    member, core = me % group, me % 2
    place = place_of(masks, member, (chips, half), 1)
    row = iota((chips, half), 0)
    wanted = (row % CAP) * (chips // CAP) + row // CAP
    select = jnp.logical_and(place == wanted, iota((chips, half), 1) % CAP == member)
    select = select.astype(F32).astype(BF16)
    same, other = [
        jnp.dot(
            select, notes[side * half : (side + 1) * half, :], preferred_element_type=F32
        )
        for side in range(2)
    ]
    early[0:chips, :] = jnp.where(core == 0, same, other)
    early[chips:, :] = jnp.where(core == 0, other, same)
    copy.wait()


def project(mine, other, early, fc_first, fc, out, rest, spread, sems):
    chips = mine.shape[0]
    devices, columns = early.shape
    pieces, step = out.shape[1:]
    ready = fc_first.shape[1] // step
    copies = [
        pltpu.make_async_copy(
            fc.at[:, pl.ds(i * step, step)], rest.at[i - ready], sems.at[i - ready]
        )
        for i in range(ready, pieces)
    ]
    for copy in copies:
        copy.start()
    core = lax.axis_index("expert") % 2
    sums = []
    for pair in ((mine, other), (other, mine)):
        total = jnp.where(core == 0, pair[0][...], pair[1][...])
        sums.append(jnp.where(core == 0, total[:, :columns], total[:, columns:]))
    inputs = (jnp.concatenate(sums, axis=0) + early[...]).astype(BF16)
    for i in range(pieces):
        if i < ready:
            block = fc_first[:, i * step : (i + 1) * step]
        else:
            copies[i - ready].wait()
            block = rest[i - ready]
        result = jnp.dot(inputs, block, preferred_element_type=F32)
        for k in range(step // LANES):
            spread[k, pl.ds(i, devices, stride=pieces), :] = result[
                :, k * LANES : (k + 1) * LANES
            ]
    turns = chips // CAP
    for c in range(2):
        for r in range(turns):
            for i in range(CAP):
                at = (c * chips + r * CAP + i) * pieces
                for k in range(step // LANES):
                    out[2 * (i * turns + r) + c, :, k * LANES : (k + 1) * LANES] = spread[
                        k, at : at + pieces, :
                    ].astype(BF16)


def finish(came, out):
    total = came[0].astype(F32)
    for d in range(1, came.shape[0]):
        total = total + came[d].astype(F32)
    step = total.shape[1]
    for i in range(total.shape[0]):
        out[:, i * step : (i + 1) * step] = total[i : i + 1].astype(BF16)


def settle(hidden, placing, came, out):
    chips = came.shape[0]
    width = out.shape[1]
    rows = jnp.concatenate(
        [came[q, :, 0:width].astype(F32) for q in range(chips)], axis=0
    ).astype(BF16)
    total = hidden[...] + jnp.dot(
        placing[...].astype(BF16), rows, preferred_element_type=F32
    )
    out[...] = total[: out.shape[0]].astype(BF16)


def far(array):
    return pltpu.with_memory_space_constraint(array, pltpu.HBM)


def near(array):
    return pltpu.with_memory_space_constraint(array, VMEM)


def early_of(notes, masks, devices, draft_rows):
    group, chips = len(masks), devices // 2
    member = lax.axis_index("expert") % group
    columns = notes.astype(F32).reshape(group, EXPERTS, group, draft_rows)
    columns = lax.dynamic_index_in_dim(columns, member, 2, keepdims=False)
    order = jnp.arange(devices)
    core, rest = order // chips, order % chips
    device = 2 * ((rest % CAP) * (chips // CAP) + rest // CAP) + core
    piece = jnp.zeros((group,), jnp.int32).at[jnp.array(masks)].set(jnp.arange(group))
    shift = (lax.axis_index("expert") // group - device // group) % EXPERTS
    return columns[piece[member ^ (device % group)], shift]


def params(mib):
    return pltpu.CompilerParams(vmem_limit_bytes=mib * MIB)


def per_device(
    queries,
    tree_key_value,
    key_value_cache,
    lengths,
    parents,
    residual,
    ffn_gain,
    router,
    routes,
    gate_weight,
    up_weight,
    down_weight,
    accepted,
    next_embed,
    draft_fc,
):
    devices = lax.axis_size("expert")
    chips = devices // 2
    group = devices // EXPERTS
    tokens, width = queries.shape
    assert lengths.shape[0] == 1 and tokens == TREE_NODES
    cache_slots, key_width = key_value_cache.shape[2:]
    hidden_units = gate_weight.shape[1]
    draft_rows = draft_fc.shape[0]
    ext = group * draft_rows // CAP
    total_width = width + ext + LANES
    same_core = [[2 * q + c for q in range(chips)] for c in range(2)]
    masks = [0]
    bits = [1 << i for i in range(group.bit_length() - 1)]
    for bit in reversed(bits):
        masks = masks + [mask | bit for mask in masks]

    def swap(array, bit):
        return lax.ppermute(array, "expert", [(d, d ^ bit) for d in range(devices)])

    first = 512 if hidden_units > 1024 else hidden_units // 2
    more = (256, 512) if hidden_units > 1024 else ()
    chunk = min(512, first)
    hidden, *parcels, placing, gate_first, up_first = pl.pallas_call(
        attend,
        out_shape=(
            jax.ShapeDtypeStruct((ROWS, width), F32),
            *[jax.ShapeDtypeStruct((CAP, total_width), BF16)] * EXPERTS,
            jax.ShapeDtypeStruct((ROWS, chips * CAP), F32),
            VMEM((width, first), BF16),
            VMEM((width, first), BF16),
        ),
        in_specs=[spec(SMEM)] * 2 + [spec(pl.ANY)] * 11,
        out_specs=(spec(VMEM),) * (4 + EXPERTS),
        scratch_shapes=[
            SMEM(parents.shape, jnp.int32),
            SMEM(routes.shape[::-1], jnp.int32),
            VMEM(queries.shape, BF16),
            VMEM(tree_key_value.shape, BF16),
            VMEM((cache_slots, key_width), BF16),
            VMEM((cache_slots, key_width), BF16),
            VMEM(residual.shape, BF16),
            VMEM((width // LANES, LANES), BF16),
            VMEM((EXPERTS, width), BF16),
            VMEM(next_embed.shape, BF16),
            VMEM((2, ROWS, key_width), F32),
            VMEM((ROWS, width), F32),
            VMEM((ROWS, width), F32),
            VMEM((EXPERTS, CAP, total_width), BF16),
            pltpu.SemaphoreType.DMA((12,)),
        ],
        compiler_params=params(12),
    )(
        lengths,
        accepted,
        far(parents),
        far(routes.T),
        far(queries),
        far(tree_key_value),
        far(key_value_cache),
        far(residual),
        far(ffn_gain.reshape(width // LANES, LANES)),
        far(router.T),
        far(next_embed),
        far(gate_weight),
        far(up_weight),
    )
    ready = [gate_first, up_first]

    def fetch_more(after, ready, more):
        at = sum(block.shape[1] for block in ready[::2])
        return ready + list(pl.pallas_call(
            functools.partial(fetch, at),
            out_shape=(VMEM((width, more), BF16), VMEM((width, more), BF16)),
            in_specs=[spec(pl.ANY)] * 3,
            out_specs=(spec(VMEM),) * 2,
            scratch_shapes=[pltpu.SemaphoreType.DMA((2,))],
            compiler_params=params(1),
            cost_estimate=pl.CostEstimate(
                flops=0, bytes_accessed=4 * width * more * 2, transcendentals=0
            ),
        )(after, far(gate_weight), far(up_weight)))

    for shift in range(1, EXPERTS):
        ring = [(d, (d + shift * group) % devices) for d in range(devices)]
        parcels[shift] = lax.ppermute(parcels[shift], "expert", ring)
    if more:
        ready = fetch_more(placing, ready, more[0])
        ready[-1], *parcels[1:] = lax.optimization_barrier((ready[-1], *parcels[1:]))
    pieces = [
        pl.pallas_call(
            join,
            out_shape=jax.ShapeDtypeStruct((EXPERTS, CAP, total_width), BF16),
            in_specs=[spec(VMEM)] * EXPERTS,
            out_specs=spec(VMEM),
            compiler_params=params(2),
        )(*parcels)
    ]
    for bit in reversed(bits[1:]):
        pieces = pieces + [swap(piece, bit) for piece in pieces]
    if more:
        ready = fetch_more(pieces[0], ready, more[1])
        ready[-1], *pieces[1:] = lax.optimization_barrier((ready[-1], *pieces[1:]))
    pieces = pieces + [swap(piece, 1) for piece in pieces]

    units = 10
    rows = 2 * chips * CAP
    padded_rows = -(-rows // 128) * 128
    keep, send, notes, weights = pl.pallas_call(
        functools.partial(experts, width, len(pieces), len(ready) // 2),
        out_shape=(
            VMEM((chips * CAP, width), F32),
            VMEM((chips * CAP, width), BF16),
            VMEM((rows, ext), BF16),
            VMEM((rows, LANES), F32),
        ),
        in_specs=[spec(VMEM)] * (len(pieces) + len(ready)) + [spec(pl.ANY)] * 3,
        out_specs=(spec(VMEM),) * 4,
        scratch_shapes=[
            VMEM((padded_rows, width), BF16),
            VMEM((padded_rows, hidden_units), BF16),
            VMEM((units, hidden_units, chunk), BF16),
            pltpu.SemaphoreType.DMA((units,)),
        ],
        compiler_params=params(25),
        cost_estimate=pl.CostEstimate(
            flops=2 * rows * width * hidden_units * 3,
            bytes_accessed=3 * down_weight.size * 2,
            transcendentals=0,
        ),
    )(
        *[near(piece) for piece in pieces],
        *[near(block) for block in ready],
        far(gate_weight),
        far(up_weight),
        far(down_weight),
    )
    came = swap(send, 1)
    fc_ready = width // 4
    fc_first, early = pl.pallas_call(
        functools.partial(draft_fetch, masks),
        out_shape=(
            VMEM((draft_rows, fc_ready), BF16),
            VMEM((devices, ext), F32),
        ),
        in_specs=[spec(VMEM), spec(pl.ANY)],
        out_specs=(spec(VMEM),) * 2,
        scratch_shapes=[pltpu.SemaphoreType.DMA((1,))],
        compiler_params=params(4),
        cost_estimate=pl.CostEstimate(
            flops=0, bytes_accessed=2 * draft_rows * fc_ready * 2, transcendentals=0
        ),
    )(near(notes), far(draft_fc))
    came, early = lax.optimization_barrier((came, early))
    span = 2 * draft_rows
    turns = chips // CAP
    partial, chosen = pl.pallas_call(
        functools.partial(combine, masks),
        out_shape=(
            jax.ShapeDtypeStruct((chips, CAP, width + turns * span), BF16),
            jax.ShapeDtypeStruct((turns, CAP, width if span % LANES else LANES), BF16),
        ),
        in_specs=[spec(VMEM)] * 3,
        out_specs=(spec(VMEM),) * 2,
        compiler_params=params(16),
    )(near(keep), came, near(weights))
    if span % LANES:
        chosen = chosen.reshape(turns, CAP, chips // 2, span).transpose(2, 1, 0, 3)
        chosen = chosen.reshape(chips // 2, CAP, turns * span)
        chosen = jnp.concatenate([chosen, jnp.zeros_like(chosen)], axis=0)
        partial = lax.dynamic_update_slice(partial, chosen, (0, 0, width))
    returned = lax.all_to_all(
        partial, "expert", 0, 0, tiled=True, axis_index_groups=same_core
    )
    if span % LANES:
        mine = jnp.sum(returned[:, :, width:].astype(F32), axis=0)
        mine = mine.reshape(CAP, turns, span).transpose(1, 0, 2).reshape(chips, span)
        early = early_of(notes, masks, devices, draft_rows)
    else:
        mine = pl.pallas_call(
            functools.partial(gather, width),
            out_shape=VMEM((chips, span), F32),
            in_specs=[spec(VMEM)],
            out_specs=spec(VMEM),
            compiler_params=params(4),
        )(returned)
    other = swap(mine, 1)
    sums = pl.pallas_call(
        project,
        out_shape=jax.ShapeDtypeStruct((devices, ROWS, width // ROWS), BF16),
        in_specs=[spec(VMEM)] * 4 + [spec(pl.ANY)],
        out_specs=spec(VMEM),
        scratch_shapes=[
            VMEM((ROWS - ROWS * fc_ready // width, draft_rows, width // ROWS), BF16),
            VMEM((width // ROWS // LANES, devices * ROWS, LANES), F32),
            pltpu.SemaphoreType.DMA((ROWS - ROWS * fc_ready // width,)),
        ],
        compiler_params=params(24),
    )(near(mine), other, near(early), near(fc_first), far(draft_fc))
    sums_came = lax.all_to_all(sums, "expert", 0, 0, tiled=True)
    layer_out = pl.pallas_call(
        settle,
        out_shape=jax.ShapeDtypeStruct((tokens, width), BF16),
        in_specs=[spec(VMEM)] * 3,
        out_specs=spec(VMEM),
        compiler_params=params(16),
    )(hidden, placing, returned)
    draft_out = pl.pallas_call(
        finish,
        out_shape=jax.ShapeDtypeStruct((1, width), BF16),
        in_specs=[spec(VMEM)],
        out_specs=spec(VMEM),
        compiler_params=params(8),
    )(sums_came)
    return (layer_out, draft_out)


def solution(mesh):
    return jax.shard_map(
        per_device,
        mesh=mesh,
        in_specs=(
            P(("groups", "expert"), None),
            P(("groups", "expert"), None, None),
            P(("groups", "expert"), None, None, None),
            P(("groups", "expert")),
            P(("groups", "expert")),
            P(("groups", "expert"), None),
            P(),
            P(),
            P(("groups", "expert"), None),
            P(None, "expert"),
            P(None, "expert"),
            P("expert", None),
            P(("groups", "expert")),
            P(("groups", "expert"), None),
            P("expert", None),
        ),
        out_specs=(P(("groups", "expert"), None), P(("groups", "expert"), None)),
        check_vma=False,
    )
```
